32 devices in a mesh: vec: 8 (over z, y), grid: 4 (over x, core).
Axes of the slice: x: 2, y: 2, z: 4, core: 2. Of those that a mesh axis runs over, the one named last changes fastest.
Arguments:
- fitting_vectors: float32 [32, 32, 1024], P('vec', 'grid'), may hold values from -6 to 6
Outputs:
- coulomb_blocks: float32 [32, 5, 4], P(('vec', 'grid'))
The draws below stay inside these ranges and needn't reach their ends.
All inputs are finite; a program needn't handle non-finite values.
Results may differ from the reference program's by a relative error of at most 0.00005.
Values sent between devices are 32-bit elements; how exact they have to be, the bound alone decides.
No kernel may reach another device: no remote copies, remote signals or barrier semaphores. Data moves between devices by JAX's collectives and lax.ppermute only.
A program may use at most 64 MiB of HBM per device.

```python
import math
import jax
import jax.numpy as jnp
from jax import lax

N = 32
PAD = 64
GROUPS = 8
VG = 4
VECTORS = 32
SHIFTS = 5


def level_of(rng, dims, split, smallest, top_value):
    def one(dim, parts):
        heights = jax.random.uniform(jax.random.fold_in(jax.random.fold_in(rng, 6), dim), (parts,), jnp.float32, smallest / len(split), top_value / len(split))
        return jnp.repeat(jnp.exp(heights), dims[dim] // parts).reshape((-1,) + (1,) * (len(dims) - dim - 1))

    factor_of = one(*split[0])
    for cut in split[1:]:
        factor_of = factor_of * one(*cut)
    return factor_of


def gaussian(stream_key, dims, deviation, limit, split=(), held_as=jnp.bfloat16):
    drawn = jax.random.normal(stream_key, dims, jnp.float32) * deviation
    if len(split) > 0:
        drawn = level_of(stream_key, dims, split, -0.22, 0.18) * drawn
    return jnp.clip(drawn, min=-limit, max=limit).astype(held_as)


def setup_inputs(seed: int = 0) -> dict:
    key_list = jax.random.split(jax.random.key(seed), 2)
    fitting_vectors = gaussian(key_list[0], (VECTORS, N, N * N), 1.0, 6.0, ((0, 8), (1, 4)), jnp.float32)
    return {"fitting_vectors": fitting_vectors}


def kernel_half(size, padded):
    full = jnp.arange(padded, dtype=jnp.int32)
    signed = jnp.where(full < padded // 2, full, full - padded).astype(jnp.float32)
    last = jnp.arange(padded // 2 + 1, dtype=jnp.int32).astype(jnp.float32)
    total_sq = (signed * signed)[:, None, None] + (signed * signed)[None, :, None] + (last * last)[None, None, :]
    wave_sq = total_sq * (2.0 * math.pi / padded) ** 2
    safe_sq = jnp.where(total_sq > 0, wave_sq, 1.0)
    half_arg = 0.5 * jnp.sqrt(safe_sq) * size
    values = 8.0 * math.pi * jnp.sin(half_arg) ** 2 / safe_sq
    anchor = 2.0 * math.pi * size * size
    return jnp.where(total_sq > 0, values, anchor)

def reference(fitting_vectors):
    kernel = kernel_half(N, PAD)

    def potential_of(field):
        cube = field.reshape(N, N, N)
        spectrum = jnp.fft.rfftn(cube, s=(PAD, PAD, PAD))
        result = jnp.fft.irfftn(spectrum * kernel, s=(PAD, PAD, PAD))[:N, :N, :N]
        return result.reshape(N, N * N)
    potentials = lax.map(potential_of, fitting_vectors)
    flat_vectors = fitting_vectors.reshape(VECTORS, -1)
    flat_potentials = potentials.reshape(VECTORS, -1)
    gram = jnp.dot(flat_vectors, flat_potentials.T, precision=lax.Precision.HIGHEST, preferred_element_type=jnp.float32) / float(N ** 3)
    row_index = jnp.arange(VECTORS, dtype=jnp.int32)[:, None, None]
    offset_index = jnp.arange(SHIFTS, dtype=jnp.int32)[None, :, None]
    within_index = jnp.arange(VG, dtype=jnp.int32)[None, None, :]
    column_index = (row_index // VG + offset_index) % GROUPS * VG + within_index
    return gram[row_index, column_index]
```

```python
import functools
import math

import jax
import jax.numpy as jnp
import numpy as np
from jax import lax
from jax.experimental import pallas as pl
from jax.experimental.pallas import tpu as pltpu
from jax.sharding import PartitionSpec as P

AXES = ("vec", "grid")
LANES = 128
ROWS = 8


def centred(size):
    return np.arange(size) - (size - 1) / 2


def pair_table(size):
    omega = math.pi / size
    freqs = np.arange(size)
    cosines = np.cos(omega * np.outer(freqs, centred(size)))
    sines = np.sin(omega * np.outer(np.where(freqs == 0, size, freqs), centred(size)))
    return np.stack([cosines, sines], 1).astype(np.float32)


def multiplicity(size):
    return np.where(np.isin(np.arange(size + 1), (0, size)), 1.0, 2.0)


def operator_spectrum(size, pair, kx_pad=0, ky_pad=0):
    kz = jnp.stack([pair, jnp.where(pair == 0, size, pair)]).astype(jnp.float32)
    times = jnp.where(pair == 0, 1.0, 2.0)
    ky = jnp.arange(size + 1 + ky_pad, dtype=jnp.int32)
    kx = jnp.arange(size + 1 + kx_pad, dtype=jnp.int32)
    fy, fx = ky.astype(jnp.float32), kx.astype(jnp.float32)
    total_sq = (kz * kz)[:, None, None] + (fy * fy)[None, :, None] + (fx * fx)[None, None, :]
    wave_sq = total_sq * (math.pi / size) ** 2
    safe_sq = jnp.where(total_sq > 0, wave_sq, 1.0)
    half_arg = 0.5 * jnp.sqrt(safe_sq) * size
    values = 8.0 * math.pi * jnp.sin(half_arg) ** 2 / safe_sq
    values = jnp.where(total_sq > 0, values, 2.0 * math.pi * size * size)

    def weight(k):
        inside = jnp.where((k == 0) | (k == size), 1.0, 2.0)
        return jnp.where(k <= size, inside, 0.0)

    scale = times / (float(2 * size) ** 3 * float(size) ** 3)
    return values * weight(ky)[None, :, None] * weight(kx)[None, None, :] * scale


def split_bf16(value):
    high = value.astype(jnp.bfloat16)
    return high, (value - high.astype(jnp.float32)).astype(jnp.bfloat16)


def split_table(table):
    table = np.asarray(table, np.float32)
    high = table.astype(jnp.bfloat16)
    return high, (table - high.astype(np.float32)).astype(jnp.bfloat16)


def analyse_kernel(size, n_grid, field_ref, table_ref, out_ref, held_ref):
    group, slab, _ = field_ref.shape
    half = size // 2
    per_block = LANES // size
    blocks = size // per_block
    lane_group = lax.broadcasted_iota(jnp.int32, (blocks * slab, LANES), 1) // size
    stacked = [
        jnp.concatenate([field_ref[v, :, b * LANES : (b + 1) * LANES] for b in range(blocks)], 0)
        for v in range(group)
    ]
    turned = []
    for q in range(per_block):
        mixed = None
        for v in range(group):
            shift = (v - q) % per_block * size
            part = pltpu.roll(stacked[v], shift, 1) if shift else stacked[v]
            mixed = part if mixed is None else jnp.where(lane_group == v, part, mixed)
        turned.append(mixed)
    for y in range(half):
        b, q = divmod(y, per_block)
        other_b, other_q = divmod(size - 1 - y, per_block)
        near = turned[q][b * slab : (b + 1) * slab]
        far = turned[other_q][other_b * slab : (other_b + 1) * slab]
        held_ref[0, y * slab : (y + 1) * slab, :] = near + far
        held_ref[1, y * slab : (y + 1) * slab, :] = near - far
    mirrored = lax.axis_index("grid") >= n_grid // 2
    for parity in range(2):
        rows = []
        for j in range(slab):
            start = jnp.where(mirrored, slab - 1 - j, j)
            rows.append(held_ref[parity, pl.ds(start, half, stride=slab), :])
        high, low = split_bf16(jnp.concatenate(rows, 0))
        operand = jnp.concatenate([high, high, low], 1)
        out_ref[:, parity * LANES : (parity + 1) * LANES] = lax.dot_general(
            table_ref[...], operand, (((1,), (1,)), ((), ())), preferred_element_type=jnp.float32
        )


def operator_kernel(size, spectrum_ref, cos_ref, wave_ref, turn_ref, high_ref, low_ref):
    half = size // 2
    width = half * half
    exact = lax.Precision.HIGHEST
    for c in range(2):
        along = jnp.dot(
            spectrum_ref[c], cos_ref[...], precision=exact, preferred_element_type=jnp.float32
        )
        for parity in range(2):
            strip = jnp.dot(
                turn_ref[parity],
                along * wave_ref[parity],
                precision=exact,
                preferred_element_type=jnp.float32,
            )

            def window(start):
                base = start // LANES * LANES
                part = strip[:, base : base + width + LANES]
                if start > base:
                    part = pltpu.roll(part, part.shape[1] - (start - base), 1)
                return part[:, :width]

            for x in range(half):
                toeplitz = window((size - 1 - x) * half)
                hankel = window(x * half)
                for sign in range(2):
                    value = 0.5 * (toeplitz - hankel if sign else toeplitz + hankel)
                    high, low = split_bf16(value)
                    high_ref[c, parity, sign, x * half : (x + 1) * half, :] = high
                    low_ref[c, parity, sign, x * half : (x + 1) * half, :] = low


def gram_kernel(n_vec, n_grid, group, got_ref, high_ref, low_ref, out_ref):
    per_tile = ROWS // group
    total = n_vec * group
    row = lax.broadcasted_iota(jnp.int32, (ROWS, got_ref.shape[2]), 0)
    left, right = [], []
    for c in range(2):
        slabs = []
        for i in range(n_grid):
            tiles = []
            for g in range(0, n_vec, 2):
                first = got_ref[g * n_grid + i]
                second = got_ref[(g + 1) * n_grid + i]
                if c == 0:
                    second = pltpu.roll(second, group, 0)
                else:
                    first = pltpu.roll(first, group, 0)
                tiles.append(jnp.where(row < group, first, second))
            slabs.append(jnp.concatenate(tiles, 0))
        for sign in range(2):
            folded = []
            for i in range(n_grid // 2):
                near, far = slabs[i], slabs[n_grid - 1 - i]
                folded.append(near - far if sign else near + far)
            for parity in range(2):
                lanes = folded[0].shape[1] // 2
                value = jnp.concatenate(
                    [f[:, parity * lanes : (parity + 1) * lanes] for f in folded], 1
                )
                high, low = split_bf16(value)
                op_high, op_low = high_ref[c, parity, sign], low_ref[c, parity, sign]
                both = jnp.dot(
                    jnp.concatenate([high, low], 0), op_high, preferred_element_type=jnp.float32
                )
                applied = both[:total] + both[total:]
                applied += jnp.dot(high, op_low, preferred_element_type=jnp.float32)
                applied_high, applied_low = split_bf16(applied)
                left += [applied_high, applied_low, applied_high]
                right += [high, high, low]
    copies = LANES // total
    gram = lax.dot_general(
        jnp.concatenate(left, 1),
        jnp.concatenate([jnp.concatenate(right, 1)] * copies, 0),
        (((1,), (1,)), ((), ())),
        preferred_element_type=jnp.float32,
    )
    owner = lax.broadcasted_iota(jnp.int32, gram.shape, 0) // group
    turned = gram
    for g in range(1, n_vec):
        turned = jnp.where(owner == g, pltpu.roll(gram, LANES - g * group, 1), turned)
    out_ref[...] = turned


def finish_kernel(got_ref, out_ref):
    _, shifts, width = out_ref.shape
    summed = jnp.sum(got_ref[...], 0, keepdims=True)
    for s in range(shifts):
        out_ref[0, s : s + 1, :] = summed[:, s * width : (s + 1) * width]


def whole_blocks(count):
    return [pl.BlockSpec(memory_space=pltpu.VMEM)] * count


def tiled_program(fitting_vectors, size, n_vec, n_grid, shifts):
    group, slab, _ = fitting_vectors.shape
    half = size // 2
    n_devices = n_vec * n_grid
    total = n_vec * group
    pair = lax.axis_index(AXES)

    spread = np.einsum("kcz,vw->kcvwz", pair_table(size), np.eye(group))
    high, low = split_table(spread.reshape(size * 2 * group, group * size))
    table = jnp.asarray(np.concatenate([high, low, high], 1))
    components = pl.pallas_call(
        functools.partial(analyse_kernel, size, n_grid),
        out_shape=jax.ShapeDtypeStruct((size * 2 * group, size * slab), jnp.float32),
        in_specs=whole_blocks(2),
        out_specs=whole_blocks(1)[0],
        scratch_shapes=[pltpu.VMEM((2, half * slab, LANES), jnp.float32)],
        name="analyse",
    )(fitting_vectors, table)
    chunks = components.reshape(n_devices, 2 * group, size * slab)
    got = lax.all_to_all(chunks, AXES, 0, 0, tiled=True)

    omega = math.pi / size
    ky_pad = -(size + 1) % ROWS
    kx_pad = -(size + 1) % LANES
    spectrum = operator_spectrum(size, pair, kx_pad, ky_pad)
    freqs_y = np.arange(size + 1 + ky_pad)
    freqs_x = np.arange(size + 1 + kx_pad)
    offsets = np.arange(-(size - 1), size + 1)
    cos_table = np.repeat(np.cos(omega * np.outer(freqs_x, offsets)), half, 1)
    angle = omega * np.outer(freqs_y, centred(size)[:half])
    waves = np.stack([np.cos(angle), np.sin(angle)])
    waves[0, size] = 0.0
    waves[1, 0] = 0.0
    op_shape = jax.ShapeDtypeStruct((2, 2, 2, half * half, half * half), jnp.bfloat16)
    op_high, op_low = pl.pallas_call(
        functools.partial(operator_kernel, size),
        out_shape=(op_shape, op_shape),
        in_specs=whole_blocks(4),
        out_specs=tuple(whole_blocks(2)),
        name="operator",
    )(
        spectrum,
        jnp.asarray(cos_table, jnp.float32),
        jnp.asarray(np.tile(waves, (1, 1, 2 * size)), jnp.float32),
        jnp.asarray(np.swapaxes(waves, 1, 2), jnp.float32),
    )

    rows = pl.pallas_call(
        functools.partial(gram_kernel, n_vec, n_grid, group),
        out_shape=jax.ShapeDtypeStruct((total, LANES), jnp.float32),
        in_specs=whole_blocks(3),
        out_specs=whole_blocks(1)[0],
        name="gram",
    )(got, op_high, op_low)
    parts = lax.all_to_all(rows, AXES, 0, 0, tiled=True)
    return pl.pallas_call(
        finish_kernel,
        out_shape=jax.ShapeDtypeStruct((1, shifts, group), jnp.float32),
        in_specs=whole_blocks(1),
        out_specs=whole_blocks(1)[0],
        name="finish",
    )(parts)


def general_program(fitting_vectors, size, n_vec, n_grid, shifts):
    exact = lax.Precision.HIGHEST
    group, slab, _ = fitting_vectors.shape
    n_devices = n_vec * n_grid
    total = n_vec * group
    rank = lax.axis_index(AXES)
    sharers = max(1, n_devices // size)
    held = max(1, size // n_devices)
    components = jnp.einsum(
        "vxyz,kcz->kcvxy",
        fitting_vectors.reshape(group, slab, size, size),
        jnp.asarray(pair_table(size)),
        precision=exact,
    )
    chunks = jnp.repeat(components, sharers, 0)
    chunks = chunks.reshape(n_devices, held, 2, group, slab, size)
    got = lax.all_to_all(chunks, AXES, 0, 0, tiled=True)
    got = got.reshape(n_vec, n_grid, held, 2, group, slab, size)
    planes = got.transpose(2, 3, 0, 4, 1, 5, 6).reshape(held, 2, total, size * size)

    omega = math.pi / size
    cells = np.arange(size)
    steps = np.cos(
        omega * (cells[:, None, None] - cells[None, :, None]) * np.arange(size + 1)
    ).astype(np.float32)
    columns = size * size // sharers
    start = rank % sharers * columns
    gram = jnp.zeros((total, total), jnp.float32)
    for h in range(held):
        spectrum = operator_spectrum(size, rank // sharers * held + h)
        along = jnp.einsum("clk,xak->clxa", spectrum, steps, precision=exact)
        operator = jnp.einsum("ybl,clxa->cxyab", steps, along, precision=exact)
        operator = operator.reshape(2, size * size, size * size)
        operator = lax.dynamic_slice_in_dim(operator, start, columns, 2)
        applied = jnp.einsum("cmp,cpq->cmq", planes[h], operator, precision=exact)
        own = lax.dynamic_slice_in_dim(planes[h], start, columns, 2)
        gram += jnp.einsum("cmq,cnq->mn", applied, own, precision=exact)
    wanted = (np.arange(n_vec)[:, None] * group + np.arange(shifts * group)) % total
    wanted = np.repeat(wanted, group, 0)
    rows = jnp.take_along_axis(gram, jnp.asarray(wanted), 1)
    rows = rows.reshape(n_devices, total // n_devices, shifts * group)
    parts = lax.all_to_all(rows, AXES, 0, 0, tiled=True)
    return jnp.sum(parts, 0).reshape(total // n_devices, shifts, group)


def body(fitting_vectors):
    n_vec, n_grid = (lax.axis_size(a) for a in AXES)
    group, slab, plane = fitting_vectors.shape
    size = math.isqrt(plane)
    shifts = n_vec // 2 + 1
    tiled = (
        n_vec * n_grid == size
        and group * size == LANES
        and slab * size == 2 * LANES
        and 2 * group == ROWS
        and n_vec * group <= LANES
        and n_vec % 2 == 0
        and n_grid % 2 == 0
        and group == n_grid
    )
    build = tiled_program if tiled else general_program
    return build(fitting_vectors, size, n_vec, n_grid, shifts)


def solution(mesh):
    return jax.shard_map(
        body,
        mesh=mesh,
        in_specs=(P("vec", "grid", None),),
        out_specs=P(("vec", "grid"), None, None),
        check_vma=False,
    )
```

```python
import functools
import math

import jax
import jax.numpy as jnp
import numpy as np
from jax import lax
from jax.experimental import pallas as pl
from jax.experimental.pallas import tpu as pltpu
from jax.sharding import PartitionSpec as P

AXES = ("vec", "grid")
LANES = 128
ROWS = 8
PARAMS = pltpu.CompilerParams(vmem_limit_bytes=16 * 2**20)


def centred(size):
    return np.arange(size) - (size - 1) / 2


def pair_table(size):
    omega = math.pi / size
    freqs = np.arange(size)
    cosines = np.cos(omega * np.outer(freqs, centred(size)))
    sines = np.sin(omega * np.outer(np.where(freqs == 0, size, freqs), centred(size)))
    return np.stack([cosines, sines], 1).astype(np.float32)


def multiplicity(size):
    return np.where(np.isin(np.arange(size + 1), (0, size)), 1.0, 2.0)


def operator_spectrum(size, pair, kx_pad=0, ky_pad=0):
    kz = jnp.stack([pair, jnp.where(pair == 0, size, pair)]).astype(jnp.float32)
    times = jnp.where(pair == 0, 1.0, 2.0)
    ky = jnp.arange(size + 1 + ky_pad, dtype=jnp.int32)
    kx = jnp.arange(size + 1 + kx_pad, dtype=jnp.int32)
    fy, fx = ky.astype(jnp.float32), kx.astype(jnp.float32)
    total_sq = (kz * kz)[:, None, None] + (fy * fy)[None, :, None] + (fx * fx)[None, None, :]
    wave_sq = total_sq * (math.pi / size) ** 2
    safe_sq = jnp.where(total_sq > 0, wave_sq, 1.0)
    half_arg = 0.5 * jnp.sqrt(safe_sq) * size
    values = 8.0 * math.pi * jnp.sin(half_arg) ** 2 / safe_sq
    values = jnp.where(total_sq > 0, values, 2.0 * math.pi * size * size)

    def weight(k):
        inside = jnp.where((k == 0) | (k == size), 1.0, 2.0)
        return jnp.where(k <= size, inside, 0.0)

    scale = times / (float(2 * size) ** 3 * float(size) ** 3)
    return values * weight(ky)[None, :, None] * weight(kx)[None, None, :] * scale


def split_bf16(value):
    high = value.astype(jnp.bfloat16)
    return high, (value - high.astype(jnp.float32)).astype(jnp.bfloat16)


def split_table(table):
    table = np.asarray(table, np.float32)
    high = table.astype(jnp.bfloat16)
    return high, (table - high.astype(np.float32)).astype(jnp.bfloat16)


def analyse_kernel(size, n_grid, field_ref, table_ref, out_ref, held_ref):
    group, slab, _ = field_ref.shape
    half = size // 2
    per_block = LANES // size
    blocks = size // per_block
    lane_group = lax.broadcasted_iota(jnp.int32, (blocks * slab, LANES), 1) // size
    stacked = [
        jnp.concatenate([field_ref[v, :, b * LANES : (b + 1) * LANES] for b in range(blocks)], 0)
        for v in range(group)
    ]
    turned = []
    for q in range(per_block):
        mixed = None
        for v in range(group):
            shift = (v - q) % per_block * size
            part = pltpu.roll(stacked[v], shift, 1) if shift else stacked[v]
            mixed = part if mixed is None else jnp.where(lane_group == v, part, mixed)
        turned.append(mixed)
    for y in range(half):
        b, q = divmod(y, per_block)
        other_b, other_q = divmod(size - 1 - y, per_block)
        near = turned[q][b * slab : (b + 1) * slab]
        far = turned[other_q][other_b * slab : (other_b + 1) * slab]
        held_ref[0, y * slab : (y + 1) * slab, :] = near + far
        held_ref[1, y * slab : (y + 1) * slab, :] = near - far
    mirrored = lax.axis_index("grid") >= n_grid // 2
    for parity in range(2):
        rows = []
        for j in range(slab):
            start = jnp.where(mirrored, slab - 1 - j, j)
            rows.append(held_ref[parity, pl.ds(start, half, stride=slab), :])
        high, low = split_bf16(jnp.concatenate(rows, 0))
        operand = jnp.concatenate([high, high, low], 1)
        values = lax.dot_general(
            table_ref[...], operand, (((1,), (1,)), ((), ())), preferred_element_type=jnp.float32
        )
        out_ref[:, parity] = values.reshape(size, 2 * group, LANES)


def operator_kernel(size, spectrum_ref, cos_ref, wave_ref, turn_ref, high_ref, low_ref):
    half = size // 2
    width = half * half
    exact = lax.Precision.HIGHEST
    for c in range(2):
        along = jnp.dot(
            spectrum_ref[c], cos_ref[...], precision=exact, preferred_element_type=jnp.float32
        )
        for parity in range(2):
            strip = jnp.dot(
                turn_ref[parity],
                along * wave_ref[parity],
                precision=exact,
                preferred_element_type=jnp.float32,
            )

            def window(start):
                base = start // LANES * LANES
                part = strip[:, base : base + width + LANES]
                if start > base:
                    part = pltpu.roll(part, part.shape[1] - (start - base), 1)
                return part[:, :width]

            for x in range(half):
                toeplitz = window((size - 1 - x) * half)
                hankel = window(x * half)
                for sign in range(2):
                    value = 0.5 * (toeplitz - hankel if sign else toeplitz + hankel)
                    high, low = split_bf16(value)
                    high_ref[c, parity, sign, x * half : (x + 1) * half, :] = high
                    low_ref[c, parity, sign, x * half : (x + 1) * half, :] = low


def gram_kernel(n_vec, n_grid, group, got_ref, high_ref, low_ref, out_ref):
    total = n_vec * group
    tile = 2 * group
    left, right = [], []
    for c in range(2):
        for parity in range(2):
            slabs = []
            for i in range(n_grid):
                start = (i * 2 + parity) * tile + c * group
                rows = [
                    got_ref[pl.ds(start + v, n_vec, stride=n_grid * 2 * tile), :]
                    for v in range(group)
                ]
                slabs.append(jnp.concatenate(rows, 0))
            for sign in range(2):
                folded = []
                for i in range(n_grid // 2):
                    near, far = slabs[i], slabs[n_grid - 1 - i]
                    folded.append(near - far if sign else near + far)
                value = jnp.concatenate(folded, 1)
                high, low = split_bf16(value)
                op_high, op_low = high_ref[c, parity, sign], low_ref[c, parity, sign]
                both = jnp.dot(
                    jnp.concatenate([high, low], 0), op_high, preferred_element_type=jnp.float32
                )
                applied = both[:total] + both[total:]
                applied += jnp.dot(high, op_low, preferred_element_type=jnp.float32)
                applied_high, applied_low = split_bf16(applied)
                left += [applied_high, applied_low, applied_high]
                right += [high, high, low]
    gram = lax.dot_general(
        jnp.concatenate(left, 1),
        jnp.concatenate([jnp.concatenate(right, 1)] * (LANES // total), 0),
        (((1,), (1,)), ((), ())),
        preferred_element_type=jnp.float32,
    )
    lane = lax.broadcasted_iota(jnp.int32, (n_vec, LANES), 1)
    row = lax.broadcasted_iota(jnp.int32, (n_vec, LANES), 0)
    for v in range(group):
        held = gram[v * n_vec : (v + 1) * n_vec]
        for w in range(group):
            start = pltpu.roll(held, LANES - w * n_vec, 1) if w else held
            wrapped = pltpu.roll(held, LANES - w * n_vec + n_vec, 1)
            period = jnp.where(lane < n_vec, start, wrapped)
            turned = period
            for g in range(1, n_vec):
                turned = jnp.where(row == g, pltpu.roll(period, LANES - g, 1), turned)
            out_ref[pl.ds(v * group + w, n_vec, stride=group * group), :] = turned


def whole_blocks(count):
    return [pl.BlockSpec(memory_space=pltpu.VMEM)] * count


def tiled_program(fitting_vectors, size, n_vec, n_grid, shifts):
    group, slab, _ = fitting_vectors.shape
    half = size // 2
    n_devices = n_vec * n_grid
    total = n_vec * group
    pair = lax.axis_index(AXES)

    spread = np.einsum("kcz,vw->kcvwz", pair_table(size), np.eye(group))
    high, low = split_table(spread.reshape(size * 2 * group, group * size))
    table = jnp.asarray(np.concatenate([high, low, high], 1))
    components = pl.pallas_call(
        functools.partial(analyse_kernel, size, n_grid),
        out_shape=jax.ShapeDtypeStruct((size, 2, 2 * group, LANES), jnp.float32),
        in_specs=whole_blocks(2),
        out_specs=whole_blocks(1)[0],
        scratch_shapes=[pltpu.VMEM((2, half * slab, LANES), jnp.float32)],
        compiler_params=PARAMS,
        name="analyse",
    )(fitting_vectors, table)
    got = lax.all_to_all(components, AXES, 0, 0, tiled=True)

    omega = math.pi / size
    ky_pad = -(size + 1) % ROWS
    kx_pad = -(size + 1) % LANES
    spectrum = operator_spectrum(size, pair, kx_pad, ky_pad)
    freqs_y = np.arange(size + 1 + ky_pad)
    freqs_x = np.arange(size + 1 + kx_pad)
    offsets = np.arange(-(size - 1), size + 1)
    cos_table = np.repeat(np.cos(omega * np.outer(freqs_x, offsets)), half, 1)
    angle = omega * np.outer(freqs_y, centred(size)[:half])
    waves = np.stack([np.cos(angle), np.sin(angle)])
    waves[0, size] = 0.0
    waves[1, 0] = 0.0
    op_shape = jax.ShapeDtypeStruct((2, 2, 2, half * half, half * half), jnp.bfloat16)
    op_high, op_low = pl.pallas_call(
        functools.partial(operator_kernel, size),
        out_shape=(op_shape, op_shape),
        in_specs=whole_blocks(4),
        out_specs=tuple(whole_blocks(2)),
        compiler_params=PARAMS,
        name="operator",
    )(
        spectrum,
        jnp.asarray(cos_table, jnp.float32),
        jnp.asarray(np.tile(waves, (1, 1, 2 * size)), jnp.float32),
        jnp.asarray(np.swapaxes(waves, 1, 2), jnp.float32),
    )

    rows = pl.pallas_call(
        functools.partial(gram_kernel, n_vec, n_grid, group),
        out_shape=jax.ShapeDtypeStruct((total * group, LANES), jnp.float32),
        in_specs=whole_blocks(3),
        out_specs=whole_blocks(1)[0],
        compiler_params=PARAMS,
        name="gram",
    )(got.reshape(n_devices * 4 * group, LANES), op_high, op_low)
    parts = lax.all_to_all(rows.reshape(total, group, LANES), AXES, 0, 0, tiled=True)
    return jnp.sum(parts[:, :, :shifts], 0).T[None]


def general_program(fitting_vectors, size, n_vec, n_grid, shifts):
    exact = lax.Precision.HIGHEST
    group, slab, _ = fitting_vectors.shape
    n_devices = n_vec * n_grid
    total = n_vec * group
    rank = lax.axis_index(AXES)
    sharers = max(1, n_devices // size)
    held = max(1, size // n_devices)
    components = jnp.einsum(
        "vxyz,kcz->kcvxy",
        fitting_vectors.reshape(group, slab, size, size),
        jnp.asarray(pair_table(size)),
        precision=exact,
    )
    chunks = jnp.repeat(components, sharers, 0)
    chunks = chunks.reshape(n_devices, held, 2, group, slab, size)
    got = lax.all_to_all(chunks, AXES, 0, 0, tiled=True)
    got = got.reshape(n_vec, n_grid, held, 2, group, slab, size)
    planes = got.transpose(2, 3, 0, 4, 1, 5, 6).reshape(held, 2, total, size * size)

    omega = math.pi / size
    cells = np.arange(size)
    steps = np.cos(
        omega * (cells[:, None, None] - cells[None, :, None]) * np.arange(size + 1)
    ).astype(np.float32)
    columns = size * size // sharers
    start = rank % sharers * columns
    gram = jnp.zeros((total, total), jnp.float32)
    for h in range(held):
        spectrum = operator_spectrum(size, rank // sharers * held + h)
        along = jnp.einsum("clk,xak->clxa", spectrum, steps, precision=exact)
        operator = jnp.einsum("ybl,clxa->cxyab", steps, along, precision=exact)
        operator = operator.reshape(2, size * size, size * size)
        operator = lax.dynamic_slice_in_dim(operator, start, columns, 2)
        applied = jnp.einsum("cmp,cpq->cmq", planes[h], operator, precision=exact)
        own = lax.dynamic_slice_in_dim(planes[h], start, columns, 2)
        gram += jnp.einsum("cmq,cnq->mn", applied, own, precision=exact)
    wanted = (np.arange(n_vec)[:, None] * group + np.arange(shifts * group)) % total
    wanted = np.repeat(wanted, group, 0)
    rows = jnp.take_along_axis(gram, jnp.asarray(wanted), 1)
    rows = rows.reshape(n_devices, total // n_devices, shifts * group)
    parts = lax.all_to_all(rows, AXES, 0, 0, tiled=True)
    return jnp.sum(parts, 0).reshape(total // n_devices, shifts, group)


def body(fitting_vectors):
    n_vec, n_grid = (lax.axis_size(a) for a in AXES)
    group, slab, plane = fitting_vectors.shape
    size = math.isqrt(plane)
    shifts = n_vec // 2 + 1
    tiled = (
        n_vec * n_grid == size
        and group * size == LANES
        and slab * size == 2 * LANES
        and 2 * group == ROWS
        and n_vec * group <= LANES
        and n_vec % 2 == 0
        and n_grid % 2 == 0
        and group == n_grid
    )
    build = tiled_program if tiled else general_program
    return build(fitting_vectors, size, n_vec, n_grid, shifts)


def solution(mesh):
    return jax.shard_map(
        body,
        mesh=mesh,
        in_specs=(P("vec", "grid", None),),
        out_specs=P(("vec", "grid"), None, None),
        check_vma=False,
    )
```

```python
import functools
import math

import jax
import jax.numpy as jnp
import numpy as np
from jax import lax
from jax.experimental import pallas as pl
from jax.experimental.pallas import tpu as pltpu
from jax.sharding import PartitionSpec as P

AXES = ("vec", "grid")
LANES = 128
ROWS = 8
PARAMS = pltpu.CompilerParams(vmem_limit_bytes=16 * 2**20)
ALL_VMEM = pltpu.CompilerParams(vmem_limit_bytes=60 * 2**20)


def centred(size):
    return np.arange(size) - (size - 1) / 2


def pair_table(size):
    omega = math.pi / size
    freqs = np.arange(size)
    cosines = np.cos(omega * np.outer(freqs, centred(size)))
    sines = np.sin(omega * np.outer(np.where(freqs == 0, size, freqs), centred(size)))
    return np.stack([cosines, sines], 1).astype(np.float32)


def multiplicity(size):
    return np.where(np.isin(np.arange(size + 1), (0, size)), 1.0, 2.0)


def operator_spectrum(size, pair, kx_pad=0, ky_pad=0):
    kz = jnp.stack([pair, jnp.where(pair == 0, size, pair)]).astype(jnp.float32)
    times = jnp.where(pair == 0, 1.0, 2.0)
    ky = jnp.arange(size + 1 + ky_pad, dtype=jnp.int32)
    kx = jnp.arange(size + 1 + kx_pad, dtype=jnp.int32)
    fy, fx = ky.astype(jnp.float32), kx.astype(jnp.float32)
    total_sq = (kz * kz)[:, None, None] + (fy * fy)[None, :, None] + (fx * fx)[None, None, :]
    wave_sq = total_sq * (math.pi / size) ** 2
    safe_sq = jnp.where(total_sq > 0, wave_sq, 1.0)
    half_arg = 0.5 * jnp.sqrt(safe_sq) * size
    values = 8.0 * math.pi * jnp.sin(half_arg) ** 2 / safe_sq
    values = jnp.where(total_sq > 0, values, 2.0 * math.pi * size * size)

    def weight(k):
        inside = jnp.where((k == 0) | (k == size), 1.0, 2.0)
        return jnp.where(k <= size, inside, 0.0)

    scale = times / (float(2 * size) ** 3 * float(size) ** 3)
    return values * weight(ky)[None, :, None] * weight(kx)[None, None, :] * scale


def split_bf16(value):
    high = value.astype(jnp.bfloat16)
    return high, (value - high.astype(jnp.float32)).astype(jnp.bfloat16)


def split_table(table):
    table = np.asarray(table, np.float32)
    high = table.astype(jnp.bfloat16)
    return high, (table - high.astype(np.float32)).astype(jnp.bfloat16)


def analyse_kernel(
    size, n_grid, field_hbm, table_hbm, out_hbm, field_ref, table_ref, held_ref, out_ref, sems
):
    group, slab, _ = field_ref.shape
    half = size // 2
    per_block = LANES // size
    blocks = size // per_block
    field_copy = pltpu.make_async_copy(field_hbm, field_ref, sems.at[0])
    table_copy = pltpu.make_async_copy(table_hbm, table_ref, sems.at[1])
    field_copy.start()
    table_copy.start()
    mirrored = lax.axis_index("grid") >= n_grid // 2
    lane_group = lax.broadcasted_iota(jnp.int32, (blocks * slab, LANES), 1) // size
    field_copy.wait()
    stacked = [
        jnp.concatenate([field_ref[v, :, b * LANES : (b + 1) * LANES] for b in range(blocks)], 0)
        for v in range(group)
    ]
    turned = []
    for q in range(per_block):
        mixed = None
        for v in range(group):
            shift = (v - q) % per_block * size
            part = pltpu.roll(stacked[v], shift, 1) if shift else stacked[v]
            mixed = part if mixed is None else jnp.where(lane_group == v, part, mixed)
        turned.append(mixed)
    for y in range(half):
        b, q = divmod(y, per_block)
        other_b, other_q = divmod(size - 1 - y, per_block)
        near = turned[q][b * slab : (b + 1) * slab]
        far = turned[other_q][other_b * slab : (other_b + 1) * slab]
        held_ref[0, y * slab : (y + 1) * slab, :] = near + far
        held_ref[1, y * slab : (y + 1) * slab, :] = near - far
    rows = []
    for parity in range(2):
        for j in range(slab):
            start = jnp.where(mirrored, slab - 1 - j, j)
            rows.append(held_ref[parity, pl.ds(start, half, stride=slab), :])
    high, low = split_bf16(jnp.concatenate(rows, 0))
    operand = jnp.concatenate([high, high, low], 1)
    table_copy.wait()
    table = jnp.concatenate([table_ref[...], table_ref[:, :LANES]], 1)
    values = lax.dot_general(
        table, operand, (((1,), (1,)), ((), ())), preferred_element_type=jnp.float32
    )
    for parity in range(2):
        part = values[:, parity * LANES : (parity + 1) * LANES]
        out_ref[:, parity] = part.reshape(size, 2 * group, LANES)
    out_copy = pltpu.make_async_copy(out_ref, out_hbm, sems.at[2])
    out_copy.start()
    out_copy.wait()


def operator_kernel(size, spectrum_ref, cos_ref, wave_ref, turn_ref, high_ref, low_ref):
    half = size // 2
    width = half * half
    exact = lax.Precision.HIGHEST
    for c in range(2):
        along = jnp.dot(
            spectrum_ref[c], cos_ref[...], precision=exact, preferred_element_type=jnp.float32
        )
        for parity in range(2):
            strip = jnp.dot(
                turn_ref[parity],
                along * wave_ref[parity],
                precision=exact,
                preferred_element_type=jnp.float32,
            )

            def window(start):
                base = start // LANES * LANES
                part = strip[:, base : base + width + LANES]
                if start > base:
                    part = pltpu.roll(part, part.shape[1] - (start - base), 1)
                return part[:, :width]

            for x in range(half):
                toeplitz = window((size - 1 - x) * half)
                hankel = window(x * half)
                for sign in range(2):
                    value = 0.5 * (toeplitz - hankel if sign else toeplitz + hankel)
                    high, low = split_bf16(value)
                    high_ref[c, parity, sign, x * half : (x + 1) * half, :] = high
                    low_ref[c, parity, sign, x * half : (x + 1) * half, :] = low


def gram_kernel(n_vec, n_grid, group, got_ref, high_ref, low_ref, out_ref):
    total = n_vec * group
    tile = 2 * group
    left, right = [], []
    for c in range(2):
        for parity in range(2):
            slabs = []
            for i in range(n_grid):
                start = (i * 2 + parity) * tile + c * group
                rows = [
                    got_ref[pl.ds(start + v, n_vec, stride=n_grid * 2 * tile), :]
                    for v in range(group)
                ]
                slabs.append(jnp.concatenate(rows, 0))
            for sign in range(2):
                folded = []
                for i in range(n_grid // 2):
                    near, far = slabs[i], slabs[n_grid - 1 - i]
                    folded.append(near - far if sign else near + far)
                value = jnp.concatenate(folded, 1)
                high, low = split_bf16(value)
                op_high, op_low = high_ref[c, parity, sign], low_ref[c, parity, sign]
                both = jnp.dot(
                    jnp.concatenate([high, low], 0), op_high, preferred_element_type=jnp.float32
                )
                applied = both[:total] + both[total:]
                applied += jnp.dot(high, op_low, preferred_element_type=jnp.float32)
                left.append(jnp.concatenate(split_bf16(applied), 0))
                right.append(jnp.concatenate([high, low], 0))
    gram = lax.dot_general(
        jnp.concatenate(left, 1),
        jnp.concatenate(right, 1),
        (((1,), (1,)), ((), ())),
        preferred_element_type=jnp.float32,
    )
    gram = gram[:total] + gram[total:]
    gram = gram[:, :total] + gram[:, total:]
    gram = jnp.concatenate([gram, jnp.zeros((total, LANES - total), jnp.float32)], 1)
    lane = lax.broadcasted_iota(jnp.int32, (n_vec, LANES), 1)
    row = lax.broadcasted_iota(jnp.int32, (n_vec, LANES), 0)
    for v in range(group):
        held = gram[v * n_vec : (v + 1) * n_vec]
        for w in range(group):
            start = pltpu.roll(held, LANES - w * n_vec, 1) if w else held
            wrapped = pltpu.roll(held, LANES - w * n_vec + n_vec, 1)
            period = jnp.where(lane < n_vec, start, wrapped)
            turned = period
            for g in range(1, n_vec):
                turned = jnp.where(row == g, pltpu.roll(period, LANES - g, 1), turned)
            out_ref[pl.ds(v * group + w, n_vec, stride=group * group), :] = turned


def whole_blocks(count):
    return [pl.BlockSpec(memory_space=pltpu.VMEM)] * count


def tiled_program(fitting_vectors, size, n_vec, n_grid, shifts):
    group, slab, _ = fitting_vectors.shape
    half = size // 2
    n_devices = n_vec * n_grid
    total = n_vec * group
    pair = lax.axis_index(AXES)

    spread = np.einsum("kcz,vw->kcvwz", pair_table(size), np.eye(group))
    high, low = split_table(spread.reshape(size * 2 * group, group * size))
    table = jnp.asarray(np.concatenate([high, low], 1))
    chunk_shape = (size, 2, 2 * group, LANES)
    components = pl.pallas_call(
        functools.partial(analyse_kernel, size, n_grid),
        out_shape=jax.ShapeDtypeStruct(chunk_shape, jnp.float32),
        in_specs=[pl.BlockSpec(memory_space=pltpu.HBM)] * 2,
        out_specs=pl.BlockSpec(memory_space=pltpu.HBM),
        scratch_shapes=[
            pltpu.VMEM(fitting_vectors.shape, jnp.float32),
            pltpu.VMEM(table.shape, table.dtype),
            pltpu.VMEM((2, half * slab, LANES), jnp.float32),
            pltpu.VMEM(chunk_shape, jnp.float32),
            pltpu.SemaphoreType.DMA((3,)),
        ],
        compiler_params=ALL_VMEM,
        name="analyse",
    )(fitting_vectors, table)
    got = lax.all_to_all(components, AXES, 0, 0, tiled=True)

    omega = math.pi / size
    ky_pad = -(size + 1) % ROWS
    kx_pad = -(size + 1) % LANES
    spectrum = operator_spectrum(size, pair, kx_pad, ky_pad)
    freqs_y = np.arange(size + 1 + ky_pad)
    freqs_x = np.arange(size + 1 + kx_pad)
    offsets = np.arange(-(size - 1), size + 1)
    cos_table = np.repeat(np.cos(omega * np.outer(freqs_x, offsets)), half, 1)
    angle = omega * np.outer(freqs_y, centred(size)[:half])
    waves = np.stack([np.cos(angle), np.sin(angle)])
    waves[0, size] = 0.0
    waves[1, 0] = 0.0
    op_shape = jax.ShapeDtypeStruct((2, 2, 2, half * half, half * half), jnp.bfloat16)
    op_high, op_low = pl.pallas_call(
        functools.partial(operator_kernel, size),
        out_shape=(op_shape, op_shape),
        in_specs=whole_blocks(4),
        out_specs=tuple(whole_blocks(2)),
        compiler_params=PARAMS,
        name="operator",
    )(
        spectrum,
        jnp.asarray(cos_table, jnp.float32),
        jnp.asarray(np.tile(waves, (1, 1, 2 * size)), jnp.float32),
        jnp.asarray(np.swapaxes(waves, 1, 2), jnp.float32),
    )

    rows = pl.pallas_call(
        functools.partial(gram_kernel, n_vec, n_grid, group),
        out_shape=jax.ShapeDtypeStruct((total * group, LANES), jnp.float32),
        in_specs=whole_blocks(3),
        out_specs=whole_blocks(1)[0],
        compiler_params=PARAMS,
        name="gram",
    )(got.reshape(n_devices * 4 * group, LANES), op_high, op_low)
    parts = lax.all_to_all(rows.reshape(total, group, LANES), AXES, 0, 0, tiled=True)
    return jnp.sum(parts[:, :, :shifts], 0).T[None]


def general_program(fitting_vectors, size, n_vec, n_grid, shifts):
    exact = lax.Precision.HIGHEST
    group, slab, _ = fitting_vectors.shape
    n_devices = n_vec * n_grid
    total = n_vec * group
    rank = lax.axis_index(AXES)
    sharers = max(1, n_devices // size)
    held = max(1, size // n_devices)
    components = jnp.einsum(
        "vxyz,kcz->kcvxy",
        fitting_vectors.reshape(group, slab, size, size),
        jnp.asarray(pair_table(size)),
        precision=exact,
    )
    chunks = jnp.repeat(components, sharers, 0)
    chunks = chunks.reshape(n_devices, held, 2, group, slab, size)
    got = lax.all_to_all(chunks, AXES, 0, 0, tiled=True)
    got = got.reshape(n_vec, n_grid, held, 2, group, slab, size)
    planes = got.transpose(2, 3, 0, 4, 1, 5, 6).reshape(held, 2, total, size * size)

    omega = math.pi / size
    cells = np.arange(size)
    steps = np.cos(
        omega * (cells[:, None, None] - cells[None, :, None]) * np.arange(size + 1)
    ).astype(np.float32)
    columns = size * size // sharers
    start = rank % sharers * columns
    gram = jnp.zeros((total, total), jnp.float32)
    for h in range(held):
        spectrum = operator_spectrum(size, rank // sharers * held + h)
        along = jnp.einsum("clk,xak->clxa", spectrum, steps, precision=exact)
        operator = jnp.einsum("ybl,clxa->cxyab", steps, along, precision=exact)
        operator = operator.reshape(2, size * size, size * size)
        operator = lax.dynamic_slice_in_dim(operator, start, columns, 2)
        applied = jnp.einsum("cmp,cpq->cmq", planes[h], operator, precision=exact)
        own = lax.dynamic_slice_in_dim(planes[h], start, columns, 2)
        gram += jnp.einsum("cmq,cnq->mn", applied, own, precision=exact)
    wanted = (np.arange(n_vec)[:, None] * group + np.arange(shifts * group)) % total
    wanted = np.repeat(wanted, group, 0)
    rows = jnp.take_along_axis(gram, jnp.asarray(wanted), 1)
    rows = rows.reshape(n_devices, total // n_devices, shifts * group)
    parts = lax.all_to_all(rows, AXES, 0, 0, tiled=True)
    return jnp.sum(parts, 0).reshape(total // n_devices, shifts, group)


def body(fitting_vectors):
    n_vec, n_grid = (lax.axis_size(a) for a in AXES)
    group, slab, plane = fitting_vectors.shape
    size = math.isqrt(plane)
    shifts = n_vec // 2 + 1
    tiled = (
        n_vec * n_grid == size
        and group * size == LANES
        and slab * size == 2 * LANES
        and 2 * group == ROWS
        and n_vec * group <= LANES
        and n_vec % 2 == 0
        and n_grid % 2 == 0
        and group == n_grid
    )
    build = tiled_program if tiled else general_program
    return build(fitting_vectors, size, n_vec, n_grid, shifts)


def solution(mesh):
    return jax.shard_map(
        body,
        mesh=mesh,
        in_specs=(P("vec", "grid", None),),
        out_specs=P(("vec", "grid"), None, None),
        check_vma=False,
    )
```

```python
import functools
import math

import jax
import jax.numpy as jnp
import numpy as np
from jax import lax
from jax.experimental import pallas as pl
from jax.experimental.pallas import tpu as pltpu
from jax.sharding import PartitionSpec as P

AXES = ("vec", "grid")
LANES = 128
ROWS = 8
PARAMS = pltpu.CompilerParams(vmem_limit_bytes=16 * 2**20)
ALL_VMEM = pltpu.CompilerParams(vmem_limit_bytes=60 * 2**20)


def centred(size):
    return np.arange(size) - (size - 1) / 2


def pair_table(size):
    omega = math.pi / size
    freqs = np.arange(size)
    cosines = np.cos(omega * np.outer(freqs, centred(size)))
    sines = np.sin(omega * np.outer(np.where(freqs == 0, size, freqs), centred(size)))
    return np.stack([cosines, sines], 1).astype(np.float32)


def multiplicity(size):
    return np.where(np.isin(np.arange(size + 1), (0, size)), 1.0, 2.0)


def operator_spectrum(size, pair, kx_pad=0, ky_pad=0):
    kz = jnp.stack([pair, jnp.where(pair == 0, size, pair)]).astype(jnp.float32)
    times = jnp.where(pair == 0, 1.0, 2.0)
    ky = jnp.arange(size + 1 + ky_pad, dtype=jnp.int32)
    kx = jnp.arange(size + 1 + kx_pad, dtype=jnp.int32)
    fy, fx = ky.astype(jnp.float32), kx.astype(jnp.float32)
    total_sq = (kz * kz)[:, None, None] + (fy * fy)[None, :, None] + (fx * fx)[None, None, :]
    wave_sq = total_sq * (math.pi / size) ** 2
    safe_sq = jnp.where(total_sq > 0, wave_sq, 1.0)
    half_arg = 0.5 * jnp.sqrt(safe_sq) * size
    values = 8.0 * math.pi * jnp.sin(half_arg) ** 2 / safe_sq
    values = jnp.where(total_sq > 0, values, 2.0 * math.pi * size * size)

    def weight(k):
        inside = jnp.where((k == 0) | (k == size), 1.0, 2.0)
        return jnp.where(k <= size, inside, 0.0)

    scale = times / (float(2 * size) ** 3 * float(size) ** 3)
    return values * weight(ky)[None, :, None] * weight(kx)[None, None, :] * scale


def split_bf16(value):
    high = value.astype(jnp.bfloat16)
    return high, (value - high.astype(jnp.float32)).astype(jnp.bfloat16)


def split_table(table):
    table = np.asarray(table, np.float32)
    high = table.astype(jnp.bfloat16)
    return high, (table - high.astype(np.float32)).astype(jnp.bfloat16)


def analyse_kernel(
    size, n_grid, field_hbm, table_hbm, out_hbm, field_ref, table_ref, held_ref, out_ref, sems
):
    group, slab, _ = field_ref.shape
    half = size // 2
    per_block = LANES // size
    blocks = size // per_block
    field_copy = pltpu.make_async_copy(field_hbm, field_ref, sems.at[0])
    table_copy = pltpu.make_async_copy(table_hbm, table_ref, sems.at[1])
    field_copy.start()
    table_copy.start()
    mirrored = lax.axis_index("grid") >= n_grid // 2
    lane_group = lax.broadcasted_iota(jnp.int32, (blocks * slab, LANES), 1) // size
    field_copy.wait()
    stacked = [
        jnp.concatenate([field_ref[v, :, b * LANES : (b + 1) * LANES] for b in range(blocks)], 0)
        for v in range(group)
    ]
    turned = []
    for q in range(per_block):
        mixed = None
        for v in range(group):
            shift = (v - q) % per_block * size
            part = pltpu.roll(stacked[v], shift, 1) if shift else stacked[v]
            mixed = part if mixed is None else jnp.where(lane_group == v, part, mixed)
        turned.append(mixed)
    for y in range(half):
        b, q = divmod(y, per_block)
        other_b, other_q = divmod(size - 1 - y, per_block)
        near = turned[q][b * slab : (b + 1) * slab]
        far = turned[other_q][other_b * slab : (other_b + 1) * slab]
        held_ref[0, y * slab : (y + 1) * slab, :] = near + far
        held_ref[1, y * slab : (y + 1) * slab, :] = near - far
    rows = []
    for parity in range(2):
        for j in range(slab):
            start = jnp.where(mirrored, slab - 1 - j, j)
            rows.append(held_ref[parity, pl.ds(start, half, stride=slab), :])
    high, low = split_bf16(jnp.concatenate(rows, 0))
    operand = jnp.concatenate([high, high, low], 1)
    table_copy.wait()
    table = jnp.concatenate([table_ref[...], table_ref[:, :LANES]], 1)
    values = lax.dot_general(
        table, operand, (((1,), (1,)), ((), ())), preferred_element_type=jnp.float32
    )
    for parity in range(2):
        part = values[:, parity * LANES : (parity + 1) * LANES]
        out_ref[:, parity] = part.reshape(size, 2 * group, LANES)
    out_copy = pltpu.make_async_copy(out_ref, out_hbm, sems.at[2])
    out_copy.start()
    out_copy.wait()


def operator_kernel(size, spectrum_ref, cos_ref, wave_ref, turn_ref, high_ref, low_ref):
    half = size // 2
    width = half * half
    exact = lax.Precision.HIGHEST
    for c in range(2):
        along = jnp.dot(
            spectrum_ref[c], cos_ref[...], precision=exact, preferred_element_type=jnp.float32
        )
        for parity in range(2):
            strip = jnp.dot(
                turn_ref[parity],
                along * wave_ref[parity],
                precision=exact,
                preferred_element_type=jnp.float32,
            )

            def window(start):
                base = start // LANES * LANES
                part = strip[:, base : base + width + LANES]
                if start > base:
                    part = pltpu.roll(part, part.shape[1] - (start - base), 1)
                return part[:, :width]

            for x in range(half):
                toeplitz = window((size - 1 - x) * half)
                hankel = window(x * half)
                for sign in range(2):
                    value = 0.5 * (toeplitz - hankel if sign else toeplitz + hankel)
                    high, low = split_bf16(value)
                    high_ref[c, parity, sign, x * half : (x + 1) * half, :] = high
                    low_ref[c, parity, sign, x * half : (x + 1) * half, :] = low


def gram_kernel(n_vec, n_grid, group, got_ref, high_ref, low_ref, out_ref):
    total = n_vec * group
    tile = 2 * group

    left, right = [], []
    for c in range(2):
        for parity in range(2):
            slabs = []
            for i in range(n_grid):
                start = (i * 2 + parity) * tile + c * group
                rows = [
                    got_ref[pl.ds(start + v, n_vec, stride=n_grid * 2 * tile), :]
                    for v in range(group)
                ]
                slabs.append(jnp.concatenate(rows, 0))
            for sign in range(2):
                folded = []
                for i in range(n_grid // 2):
                    near, far = slabs[i], slabs[n_grid - 1 - i]
                    folded.append(near - far if sign else near + far)
                value = jnp.concatenate(folded, 1)
                high, low = split_bf16(value)
                op_high, op_low = high_ref[c, parity, sign], low_ref[c, parity, sign]
                both = jnp.dot(
                    jnp.concatenate([high, low], 0), op_high, preferred_element_type=jnp.float32
                )
                applied = both[:total] + both[total:]
                applied += jnp.dot(high, op_low, preferred_element_type=jnp.float32)
                left.append(jnp.concatenate(split_bf16(applied), 0))
                right.append(jnp.concatenate([high, low], 0))
    gram = lax.dot_general(
        jnp.concatenate(left, 1),
        jnp.concatenate(right, 1),
        (((1,), (1,)), ((), ())),
        preferred_element_type=jnp.float32,
    )
    gram = gram[:total] + gram[total:]
    gram = jnp.concatenate([gram, jnp.zeros((total, LANES - 2 * total), jnp.float32)], 1)
    gram += pltpu.roll(gram, LANES - total, 1)
    owner = lax.broadcasted_iota(jnp.int32, gram.shape, 0) % n_vec
    place = lax.broadcasted_iota(jnp.int32, gram.shape, 1) % n_vec
    step = 1
    while step < n_vec:
        ahead = pltpu.roll(gram, LANES - step, 1)
        behind = pltpu.roll(gram, n_vec - step, 1)
        turned = jnp.where(place < n_vec - step, ahead, behind)
        gram = jnp.where(owner // step % 2 == 1, turned, gram)
        step *= 2
    for w in range(group):
        turned = pltpu.roll(gram, LANES - w * n_vec, 1) if w else gram
        for v in range(group):
            out_ref[pl.ds(v * group + w, n_vec, stride=group * group), :] = turned[
                v * n_vec : (v + 1) * n_vec
            ]


def whole_blocks(count):
    return [pl.BlockSpec(memory_space=pltpu.VMEM)] * count


def tiled_program(fitting_vectors, size, n_vec, n_grid, shifts):
    group, slab, _ = fitting_vectors.shape
    half = size // 2
    n_devices = n_vec * n_grid
    total = n_vec * group
    pair = lax.axis_index(AXES)

    spread = np.einsum("kcz,vw->kcvwz", pair_table(size), np.eye(group))
    high, low = split_table(spread.reshape(size * 2 * group, group * size))
    table = jnp.asarray(np.concatenate([high, low], 1))
    chunk_shape = (size, 2, 2 * group, LANES)
    components = pl.pallas_call(
        functools.partial(analyse_kernel, size, n_grid),
        out_shape=jax.ShapeDtypeStruct(chunk_shape, jnp.float32),
        in_specs=[pl.BlockSpec(memory_space=pltpu.HBM)] * 2,
        out_specs=pl.BlockSpec(memory_space=pltpu.HBM),
        scratch_shapes=[
            pltpu.VMEM(fitting_vectors.shape, jnp.float32),
            pltpu.VMEM(table.shape, table.dtype),
            pltpu.VMEM((2, half * slab, LANES), jnp.float32),
            pltpu.VMEM(chunk_shape, jnp.float32),
            pltpu.SemaphoreType.DMA((3,)),
        ],
        compiler_params=ALL_VMEM,
        name="analyse",
    )(fitting_vectors, table)
    got = lax.all_to_all(components, AXES, 0, 0, tiled=True)

    omega = math.pi / size
    ky_pad = -(size + 1) % ROWS
    kx_pad = -(size + 1) % ROWS
    spectrum = operator_spectrum(size, pair, kx_pad, ky_pad)
    freqs_y = np.arange(size + 1 + ky_pad)
    freqs_x = np.arange(size + 1 + kx_pad)
    offsets = np.arange(-(size - 1), size + 1)
    cos_table = np.repeat(np.cos(omega * np.outer(freqs_x, offsets)), half, 1)
    angle = omega * np.outer(freqs_y, centred(size)[:half])
    waves = np.stack([np.cos(angle), np.sin(angle)])
    waves[0, size] = 0.0
    waves[1, 0] = 0.0
    op_shape = jax.ShapeDtypeStruct((2, 2, 2, half * half, half * half), jnp.bfloat16)
    op_high, op_low = pl.pallas_call(
        functools.partial(operator_kernel, size),
        out_shape=(op_shape, op_shape),
        in_specs=whole_blocks(4),
        out_specs=tuple(whole_blocks(2)),
        compiler_params=PARAMS,
        name="operator",
    )(
        spectrum,
        jnp.asarray(cos_table, jnp.float32),
        jnp.asarray(np.tile(waves, (1, 1, 2 * size)), jnp.float32),
        jnp.asarray(np.swapaxes(waves, 1, 2), jnp.float32),
    )

    rows = pl.pallas_call(
        functools.partial(gram_kernel, n_vec, n_grid, group),
        out_shape=jax.ShapeDtypeStruct((total * group, LANES), jnp.float32),
        in_specs=whole_blocks(3),
        out_specs=whole_blocks(1)[0],
        compiler_params=PARAMS,
        name="gram",
    )(got.reshape(n_devices * 4 * group, LANES), op_high, op_low)
    parts = lax.all_to_all(rows.reshape(total, group, LANES), AXES, 0, 0, tiled=True)
    return jnp.sum(parts[:, :, :shifts], 0).T[None]


def general_program(fitting_vectors, size, n_vec, n_grid, shifts):
    exact = lax.Precision.HIGHEST
    group, slab, _ = fitting_vectors.shape
    n_devices = n_vec * n_grid
    total = n_vec * group
    rank = lax.axis_index(AXES)
    sharers = max(1, n_devices // size)
    held = max(1, size // n_devices)
    components = jnp.einsum(
        "vxyz,kcz->kcvxy",
        fitting_vectors.reshape(group, slab, size, size),
        jnp.asarray(pair_table(size)),
        precision=exact,
    )
    chunks = jnp.repeat(components, sharers, 0)
    chunks = chunks.reshape(n_devices, held, 2, group, slab, size)
    got = lax.all_to_all(chunks, AXES, 0, 0, tiled=True)
    got = got.reshape(n_vec, n_grid, held, 2, group, slab, size)
    planes = got.transpose(2, 3, 0, 4, 1, 5, 6).reshape(held, 2, total, size * size)

    omega = math.pi / size
    cells = np.arange(size)
    steps = np.cos(
        omega * (cells[:, None, None] - cells[None, :, None]) * np.arange(size + 1)
    ).astype(np.float32)
    columns = size * size // sharers
    start = rank % sharers * columns
    gram = jnp.zeros((total, total), jnp.float32)
    for h in range(held):
        spectrum = operator_spectrum(size, rank // sharers * held + h)
        along = jnp.einsum("clk,xak->clxa", spectrum, steps, precision=exact)
        operator = jnp.einsum("ybl,clxa->cxyab", steps, along, precision=exact)
        operator = operator.reshape(2, size * size, size * size)
        operator = lax.dynamic_slice_in_dim(operator, start, columns, 2)
        applied = jnp.einsum("cmp,cpq->cmq", planes[h], operator, precision=exact)
        own = lax.dynamic_slice_in_dim(planes[h], start, columns, 2)
        gram += jnp.einsum("cmq,cnq->mn", applied, own, precision=exact)
    wanted = (np.arange(n_vec)[:, None] * group + np.arange(shifts * group)) % total
    wanted = np.repeat(wanted, group, 0)
    rows = jnp.take_along_axis(gram, jnp.asarray(wanted), 1)
    rows = rows.reshape(n_devices, total // n_devices, shifts * group)
    parts = lax.all_to_all(rows, AXES, 0, 0, tiled=True)
    return jnp.sum(parts, 0).reshape(total // n_devices, shifts, group)


def body(fitting_vectors):
    n_vec, n_grid = (lax.axis_size(a) for a in AXES)
    group, slab, plane = fitting_vectors.shape
    size = math.isqrt(plane)
    shifts = n_vec // 2 + 1
    tiled = (
        n_vec * n_grid == size
        and group * size == LANES
        and slab * size == 2 * LANES
        and 2 * group == ROWS
        and n_vec * group <= LANES
        and n_vec % 2 == 0
        and n_grid % 2 == 0
        and group == n_grid
    )
    build = tiled_program if tiled else general_program
    return build(fitting_vectors, size, n_vec, n_grid, shifts)


def solution(mesh):
    return jax.shard_map(
        body,
        mesh=mesh,
        in_specs=(P("vec", "grid", None),),
        out_specs=P(("vec", "grid"), None, None),
        check_vma=False,
    )
```

```python
import functools
import math

import jax
import jax.numpy as jnp
import numpy as np
from jax import lax
from jax.experimental import pallas as pl
from jax.experimental.pallas import tpu as pltpu
from jax.sharding import PartitionSpec as P

AXES = ("vec", "grid")
LANES = 128
ROWS = 8
OUT_COPIES = 4
PARAMS = pltpu.CompilerParams(vmem_limit_bytes=16 * 2**20)
ALL_VMEM = pltpu.CompilerParams(vmem_limit_bytes=60 * 2**20)


def centred(size):
    return np.arange(size) - (size - 1) / 2


def pair_table(size):
    omega = math.pi / size
    freqs = np.arange(size)
    cosines = np.cos(omega * np.outer(freqs, centred(size)))
    sines = np.sin(omega * np.outer(np.where(freqs == 0, size, freqs), centred(size)))
    return np.stack([cosines, sines], 1).astype(np.float32)


def multiplicity(size):
    return np.where(np.isin(np.arange(size + 1), (0, size)), 1.0, 2.0)


def operator_spectrum(size, pair, kx_pad=0, ky_pad=0):
    kz = jnp.stack([pair, jnp.where(pair == 0, size, pair)]).astype(jnp.float32)
    times = jnp.where(pair == 0, 1.0, 2.0)
    ky = jnp.arange(size + 1 + ky_pad, dtype=jnp.int32)
    kx = jnp.arange(size + 1 + kx_pad, dtype=jnp.int32)
    fy, fx = ky.astype(jnp.float32), kx.astype(jnp.float32)
    total_sq = (kz * kz)[:, None, None] + (fy * fy)[None, :, None] + (fx * fx)[None, None, :]
    wave_sq = total_sq * (math.pi / size) ** 2
    safe_sq = jnp.where(total_sq > 0, wave_sq, 1.0)
    half_arg = 0.5 * jnp.sqrt(safe_sq) * size
    values = 8.0 * math.pi * jnp.sin(half_arg) ** 2 / safe_sq
    values = jnp.where(total_sq > 0, values, 2.0 * math.pi * size * size)

    def weight(k):
        inside = jnp.where((k == 0) | (k == size), 1.0, 2.0)
        return jnp.where(k <= size, inside, 0.0)

    scale = times / (float(2 * size) ** 3 * float(size) ** 3)
    return values * weight(ky)[None, :, None] * weight(kx)[None, None, :] * scale


def split_bf16(value):
    high = value.astype(jnp.bfloat16)
    return high, (value - high.astype(jnp.float32)).astype(jnp.bfloat16)


def split_table(table):
    table = np.asarray(table, np.float32)
    high = table.astype(jnp.bfloat16)
    return high, (table - high.astype(np.float32)).astype(jnp.bfloat16)


def analyse_kernel(
    size, n_grid, field_hbm, table_hbm, out_hbm, field_ref, table_ref, held_ref, out_ref, sems
):
    group, slab, _ = field_ref.shape
    half = size // 2
    per_block = LANES // size
    blocks = size // per_block
    field_copies = [
        pltpu.make_async_copy(field_hbm.at[v], field_ref.at[v], sems.at[v]) for v in range(group)
    ]
    table_copy = pltpu.make_async_copy(table_hbm, table_ref, sems.at[group])
    for copy in field_copies:
        copy.start()
    table_copy.start()
    mirrored = lax.axis_index("grid") >= n_grid // 2
    lane_group = lax.broadcasted_iota(jnp.int32, (blocks * slab, LANES), 1) // size
    for copy in field_copies:
        copy.wait()
    stacked = [
        jnp.concatenate([field_ref[v, :, b * LANES : (b + 1) * LANES] for b in range(blocks)], 0)
        for v in range(group)
    ]
    turned = []
    for q in range(per_block):
        mixed = None
        for v in range(group):
            shift = (v - q) % per_block * size
            part = pltpu.roll(stacked[v], shift, 1) if shift else stacked[v]
            mixed = part if mixed is None else jnp.where(lane_group == v, part, mixed)
        turned.append(mixed)
    for y in range(half):
        b, q = divmod(y, per_block)
        other_b, other_q = divmod(size - 1 - y, per_block)
        near = turned[q][b * slab : (b + 1) * slab]
        far = turned[other_q][other_b * slab : (other_b + 1) * slab]
        held_ref[0, y * slab : (y + 1) * slab, :] = near + far
        held_ref[1, y * slab : (y + 1) * slab, :] = near - far
    rows = []
    for parity in range(2):
        for j in range(slab):
            start = jnp.where(mirrored, slab - 1 - j, j)
            rows.append(held_ref[parity, pl.ds(start, half, stride=slab), :])
    high, low = split_bf16(jnp.concatenate(rows, 0))
    operand = jnp.concatenate([high, high, low], 1)
    table_copy.wait()
    table = jnp.concatenate([table_ref[...], table_ref[:, :LANES]], 1)
    values = lax.dot_general(
        table, operand, (((1,), (1,)), ((), ())), preferred_element_type=jnp.float32
    )
    parts = sems.shape[0] - group - 1
    step = size // parts
    out_copies = []
    for p in range(parts):
        rows = slice(p * step * 2 * group, (p + 1) * step * 2 * group)
        own = slice(p * step, (p + 1) * step)
        for parity in range(2):
            part = values[rows, parity * LANES : (parity + 1) * LANES]
            out_ref[own, parity] = part.reshape(step, 2 * group, LANES)
        copy = pltpu.make_async_copy(out_ref.at[own], out_hbm.at[own], sems.at[group + 1 + p])
        copy.start()
        out_copies.append(copy)
    for copy in out_copies:
        copy.wait()


def operator_kernel(size, spectrum_ref, cos_ref, wave_ref, turn_ref, high_ref, low_ref):
    half = size // 2
    width = half * half
    exact = lax.Precision.HIGHEST
    for c in range(2):
        along = jnp.dot(
            spectrum_ref[c], cos_ref[...], precision=exact, preferred_element_type=jnp.float32
        )
        for parity in range(2):
            strip = jnp.dot(
                turn_ref[parity],
                along * wave_ref[parity],
                precision=exact,
                preferred_element_type=jnp.float32,
            )

            def window(start):
                base = start // LANES * LANES
                part = strip[:, base : base + width + LANES]
                if start > base:
                    part = pltpu.roll(part, part.shape[1] - (start - base), 1)
                return part[:, :width]

            for x in range(half):
                toeplitz = window((size - 1 - x) * half)
                hankel = window(x * half)
                for sign in range(2):
                    value = 0.5 * (toeplitz - hankel if sign else toeplitz + hankel)
                    high, low = split_bf16(value)
                    high_ref[c, parity, sign, x * half : (x + 1) * half, :] = high
                    low_ref[c, parity, sign, x * half : (x + 1) * half, :] = low


def gram_kernel(n_vec, n_grid, group, got_ref, high_ref, low_ref, out_ref):
    total = n_vec * group
    tile = 2 * group

    left, right = [], []
    for c in range(2):
        for parity in range(2):
            slabs = []
            for i in range(n_grid):
                start = (i * 2 + parity) * tile + c * group
                rows = [
                    got_ref[pl.ds(start + v, n_vec, stride=n_grid * 2 * tile), :]
                    for v in range(group)
                ]
                slabs.append(jnp.concatenate(rows, 0))
            for sign in range(2):
                folded = []
                for i in range(n_grid // 2):
                    near, far = slabs[i], slabs[n_grid - 1 - i]
                    folded.append(near - far if sign else near + far)
                value = jnp.concatenate(folded, 1)
                high, low = split_bf16(value)
                op_high, op_low = high_ref[c, parity, sign], low_ref[c, parity, sign]
                both = jnp.dot(
                    jnp.concatenate([high, low], 0), op_high, preferred_element_type=jnp.float32
                )
                applied = both[:total] + both[total:]
                applied += jnp.dot(high, op_low, preferred_element_type=jnp.float32)
                left.append(jnp.concatenate(split_bf16(applied), 0))
                right.append(jnp.concatenate([high, low], 0))
    gram = lax.dot_general(
        jnp.concatenate(left, 1),
        jnp.concatenate(right, 1),
        (((1,), (1,)), ((), ())),
        preferred_element_type=jnp.float32,
    )
    gram = gram[:total] + gram[total:]
    gram = jnp.concatenate([gram, jnp.zeros((total, LANES - 2 * total), jnp.float32)], 1)
    gram += pltpu.roll(gram, LANES - total, 1)
    owner = lax.broadcasted_iota(jnp.int32, gram.shape, 0) % n_vec
    place = lax.broadcasted_iota(jnp.int32, gram.shape, 1) % n_vec
    step = 1
    while step < n_vec:
        ahead = pltpu.roll(gram, LANES - step, 1)
        behind = pltpu.roll(gram, n_vec - step, 1)
        turned = jnp.where(place < n_vec - step, ahead, behind)
        gram = jnp.where(owner // step % 2 == 1, turned, gram)
        step *= 2
    for v in range(group):
        out_ref[pl.ds(v, n_vec, stride=group), :] = gram[v * n_vec : (v + 1) * n_vec]


def finish_kernel(n_vec, got_ref, out_ref):
    _, group, shifts = out_ref.shape
    summed = jnp.sum(got_ref[...], 0, keepdims=True)
    for w in range(group):
        turned = pltpu.roll(summed, LANES - w * n_vec, 1) if w else summed
        out_ref[0, w : w + 1, :] = turned[:, :shifts]


def whole_blocks(count):
    return [pl.BlockSpec(memory_space=pltpu.VMEM)] * count


def tiled_program(fitting_vectors, size, n_vec, n_grid, shifts):
    group, slab, _ = fitting_vectors.shape
    half = size // 2
    n_devices = n_vec * n_grid
    total = n_vec * group
    pair = lax.axis_index(AXES)

    spread = np.einsum("kcz,vw->kcvwz", pair_table(size), np.eye(group))
    high, low = split_table(spread.reshape(size * 2 * group, group * size))
    table = jnp.asarray(np.concatenate([high, low], 1))
    chunk_shape = (size, 2, 2 * group, LANES)
    components = pl.pallas_call(
        functools.partial(analyse_kernel, size, n_grid),
        out_shape=jax.ShapeDtypeStruct(chunk_shape, jnp.float32),
        in_specs=[pl.BlockSpec(memory_space=pltpu.HBM)] * 2,
        out_specs=pl.BlockSpec(memory_space=pltpu.HBM),
        scratch_shapes=[
            pltpu.VMEM(fitting_vectors.shape, jnp.float32),
            pltpu.VMEM(table.shape, table.dtype),
            pltpu.VMEM((2, half * slab, LANES), jnp.float32),
            pltpu.VMEM(chunk_shape, jnp.float32),
            pltpu.SemaphoreType.DMA((group + 1 + OUT_COPIES,)),
        ],
        compiler_params=ALL_VMEM,
        name="analyse",
    )(fitting_vectors, table)
    got = lax.all_to_all(components, AXES, 0, 0, tiled=True)

    omega = math.pi / size
    ky_pad = -(size + 1) % ROWS
    kx_pad = -(size + 1) % ROWS
    spectrum = operator_spectrum(size, pair, kx_pad, ky_pad)
    freqs_y = np.arange(size + 1 + ky_pad)
    freqs_x = np.arange(size + 1 + kx_pad)
    offsets = np.arange(-(size - 1), size + 1)
    cos_table = np.repeat(np.cos(omega * np.outer(freqs_x, offsets)), half, 1)
    angle = omega * np.outer(freqs_y, centred(size)[:half])
    waves = np.stack([np.cos(angle), np.sin(angle)])
    waves[0, size] = 0.0
    waves[1, 0] = 0.0
    op_shape = jax.ShapeDtypeStruct((2, 2, 2, half * half, half * half), jnp.bfloat16)
    op_high, op_low = pl.pallas_call(
        functools.partial(operator_kernel, size),
        out_shape=(op_shape, op_shape),
        in_specs=whole_blocks(4),
        out_specs=tuple(whole_blocks(2)),
        compiler_params=PARAMS,
        name="operator",
    )(
        spectrum,
        jnp.asarray(cos_table, jnp.float32),
        jnp.asarray(np.tile(waves, (1, 1, 2 * size)), jnp.float32),
        jnp.asarray(np.swapaxes(waves, 1, 2), jnp.float32),
    )

    rows = pl.pallas_call(
        functools.partial(gram_kernel, n_vec, n_grid, group),
        out_shape=jax.ShapeDtypeStruct((total, LANES), jnp.float32),
        in_specs=whole_blocks(3),
        out_specs=whole_blocks(1)[0],
        compiler_params=PARAMS,
        name="gram",
    )(got.reshape(n_devices * 4 * group, LANES), op_high, op_low)
    parts = lax.all_to_all(rows, AXES, 0, 0, tiled=True)
    return pl.pallas_call(
        functools.partial(finish_kernel, n_vec),
        out_shape=jax.ShapeDtypeStruct((1, group, shifts), jnp.float32),
        in_specs=whole_blocks(1),
        out_specs=whole_blocks(1)[0],
        compiler_params=PARAMS,
        name="finish",
    )(parts).transpose(0, 2, 1)


def general_program(fitting_vectors, size, n_vec, n_grid, shifts):
    exact = lax.Precision.HIGHEST
    group, slab, _ = fitting_vectors.shape
    n_devices = n_vec * n_grid
    total = n_vec * group
    rank = lax.axis_index(AXES)
    sharers = max(1, n_devices // size)
    held = max(1, size // n_devices)
    components = jnp.einsum(
        "vxyz,kcz->kcvxy",
        fitting_vectors.reshape(group, slab, size, size),
        jnp.asarray(pair_table(size)),
        precision=exact,
    )
    chunks = jnp.repeat(components, sharers, 0)
    chunks = chunks.reshape(n_devices, held, 2, group, slab, size)
    got = lax.all_to_all(chunks, AXES, 0, 0, tiled=True)
    got = got.reshape(n_vec, n_grid, held, 2, group, slab, size)
    planes = got.transpose(2, 3, 0, 4, 1, 5, 6).reshape(held, 2, total, size * size)

    omega = math.pi / size
    cells = np.arange(size)
    steps = np.cos(
        omega * (cells[:, None, None] - cells[None, :, None]) * np.arange(size + 1)
    ).astype(np.float32)
    columns = size * size // sharers
    start = rank % sharers * columns
    gram = jnp.zeros((total, total), jnp.float32)
    for h in range(held):
        spectrum = operator_spectrum(size, rank // sharers * held + h)
        along = jnp.einsum("clk,xak->clxa", spectrum, steps, precision=exact)
        operator = jnp.einsum("ybl,clxa->cxyab", steps, along, precision=exact)
        operator = operator.reshape(2, size * size, size * size)
        operator = lax.dynamic_slice_in_dim(operator, start, columns, 2)
        applied = jnp.einsum("cmp,cpq->cmq", planes[h], operator, precision=exact)
        own = lax.dynamic_slice_in_dim(planes[h], start, columns, 2)
        gram += jnp.einsum("cmq,cnq->mn", applied, own, precision=exact)
    wanted = (np.arange(n_vec)[:, None] * group + np.arange(shifts * group)) % total
    wanted = np.repeat(wanted, group, 0)
    rows = jnp.take_along_axis(gram, jnp.asarray(wanted), 1)
    rows = rows.reshape(n_devices, total // n_devices, shifts * group)
    parts = lax.all_to_all(rows, AXES, 0, 0, tiled=True)
    return jnp.sum(parts, 0).reshape(total // n_devices, shifts, group)


def body(fitting_vectors):
    n_vec, n_grid = (lax.axis_size(a) for a in AXES)
    group, slab, plane = fitting_vectors.shape
    size = math.isqrt(plane)
    shifts = n_vec // 2 + 1
    tiled = (
        n_vec * n_grid == size
        and group * size == LANES
        and slab * size == 2 * LANES
        and 2 * group == ROWS
        and n_vec * group <= LANES
        and n_vec % 2 == 0
        and n_grid % 2 == 0
        and group == n_grid
    )
    build = tiled_program if tiled else general_program
    return build(fitting_vectors, size, n_vec, n_grid, shifts)


def solution(mesh):
    return jax.shard_map(
        body,
        mesh=mesh,
        in_specs=(P("vec", "grid", None),),
        out_specs=P(("vec", "grid"), None, None),
        check_vma=False,
    )
```

```python
import functools
import math

import jax
import jax.numpy as jnp
import numpy as np
from jax import lax
from jax.experimental import pallas as pl
from jax.experimental.pallas import tpu as pltpu
from jax.sharding import PartitionSpec as P

AXES = ("vec", "grid")
LANES = 128
ROWS = 8
OUT_COPIES = 4
PARAMS = pltpu.CompilerParams(vmem_limit_bytes=16 * 2**20)
ALL_VMEM = pltpu.CompilerParams(vmem_limit_bytes=60 * 2**20)


def centred(size):
    return np.arange(size) - (size - 1) / 2


def pair_table(size):
    omega = math.pi / size
    freqs = np.arange(size)
    cosines = np.cos(omega * np.outer(freqs, centred(size)))
    sines = np.sin(omega * np.outer(np.where(freqs == 0, size, freqs), centred(size)))
    return np.stack([cosines, sines], 1).astype(np.float32)


def multiplicity(size):
    return np.where(np.isin(np.arange(size + 1), (0, size)), 1.0, 2.0)


def operator_spectrum(size, pair, kx_pad=0, ky_pad=0):
    kz = jnp.stack([pair, jnp.where(pair == 0, size, pair)]).astype(jnp.float32)
    times = jnp.where(pair == 0, 1.0, 2.0)
    ky = jnp.arange(size + 1 + ky_pad, dtype=jnp.int32)
    kx = jnp.arange(size + 1 + kx_pad, dtype=jnp.int32)
    fy, fx = ky.astype(jnp.float32), kx.astype(jnp.float32)
    total_sq = (kz * kz)[:, None, None] + (fy * fy)[None, :, None] + (fx * fx)[None, None, :]
    wave_sq = total_sq * (math.pi / size) ** 2
    safe_sq = jnp.where(total_sq > 0, wave_sq, 1.0)
    half_arg = 0.5 * jnp.sqrt(safe_sq) * size
    values = 8.0 * math.pi * jnp.sin(half_arg) ** 2 / safe_sq
    values = jnp.where(total_sq > 0, values, 2.0 * math.pi * size * size)

    def weight(k):
        inside = jnp.where((k == 0) | (k == size), 1.0, 2.0)
        return jnp.where(k <= size, inside, 0.0)

    scale = times / (float(2 * size) ** 3 * float(size) ** 3)
    return values * weight(ky)[None, :, None] * weight(kx)[None, None, :] * scale


def split_bf16(value):
    high = value.astype(jnp.bfloat16)
    return high, (value - high.astype(jnp.float32)).astype(jnp.bfloat16)


def split_table(table):
    table = np.asarray(table, np.float32)
    high = table.astype(jnp.bfloat16)
    return high, (table - high.astype(np.float32)).astype(jnp.bfloat16)


def analyse_kernel(
    size, n_grid, field_hbm, table_hbm, out_hbm, field_ref, table_ref, held_ref, out_ref, sems
):
    group, slab, _ = field_ref.shape
    half = size // 2
    per_block = LANES // size
    blocks = size // per_block
    field_copies = [
        pltpu.make_async_copy(field_hbm.at[v], field_ref.at[v], sems.at[v]) for v in range(group)
    ]
    table_copy = pltpu.make_async_copy(table_hbm, table_ref, sems.at[group])
    for copy in field_copies:
        copy.start()
    table_copy.start()
    mirrored = lax.axis_index("grid") >= n_grid // 2
    lane_group = lax.broadcasted_iota(jnp.int32, (blocks * slab, LANES), 1) // size
    for copy in field_copies:
        copy.wait()
    stacked = [
        jnp.concatenate([field_ref[v, :, b * LANES : (b + 1) * LANES] for b in range(blocks)], 0)
        for v in range(group)
    ]
    turned = []
    for q in range(per_block):
        mixed = None
        for v in range(group):
            shift = (v - q) % per_block * size
            part = pltpu.roll(stacked[v], shift, 1) if shift else stacked[v]
            mixed = part if mixed is None else jnp.where(lane_group == v, part, mixed)
        turned.append(mixed)
    for y in range(half):
        b, q = divmod(y, per_block)
        other_b, other_q = divmod(size - 1 - y, per_block)
        near = turned[q][b * slab : (b + 1) * slab]
        far = turned[other_q][other_b * slab : (other_b + 1) * slab]
        held_ref[0, y * slab : (y + 1) * slab, :] = near + far
        held_ref[1, y * slab : (y + 1) * slab, :] = near - far
    rows = []
    for parity in range(2):
        for j in range(slab):
            start = jnp.where(mirrored, slab - 1 - j, j)
            rows.append(held_ref[parity, pl.ds(start, half, stride=slab), :])
    high, low = split_bf16(jnp.concatenate(rows, 0))
    operand = jnp.concatenate([high, high, low], 1)
    table_copy.wait()
    table = jnp.concatenate([table_ref[...], table_ref[:, :LANES]], 1)
    values = lax.dot_general(
        table, operand, (((1,), (1,)), ((), ())), preferred_element_type=jnp.float32
    )
    parts = sems.shape[0] - group - 1
    step = size // parts
    out_copies = []
    for p in range(parts):
        rows = slice(p * step * 2 * group, (p + 1) * step * 2 * group)
        own = slice(p * step, (p + 1) * step)
        for parity in range(2):
            part = values[rows, parity * LANES : (parity + 1) * LANES]
            out_ref[own, parity] = part.reshape(step, 2 * group, LANES)
        copy = pltpu.make_async_copy(out_ref.at[own], out_hbm.at[own], sems.at[group + 1 + p])
        copy.start()
        out_copies.append(copy)
    for copy in out_copies:
        copy.wait()


def operator_kernel(size, spectrum_ref, cos_ref, wave_ref, turn_ref, high_ref, low_ref):
    half = size // 2
    width = half * half
    exact = lax.Precision.HIGHEST
    for c in range(2):
        along = jnp.dot(
            spectrum_ref[c], cos_ref[...], precision=exact, preferred_element_type=jnp.float32
        )
        for parity in range(2):
            strip = jnp.dot(
                turn_ref[parity],
                along * wave_ref[parity],
                precision=exact,
                preferred_element_type=jnp.float32,
            )

            def window(start):
                base = start // LANES * LANES
                part = strip[:, base : base + width + LANES]
                if start > base:
                    part = pltpu.roll(part, part.shape[1] - (start - base), 1)
                return part[:, :width]

            for x in range(half):
                toeplitz = window((size - 1 - x) * half)
                hankel = window(x * half)
                for sign in range(2):
                    value = 0.5 * (toeplitz - hankel if sign else toeplitz + hankel)
                    high, low = split_bf16(value)
                    high_ref[c, parity, sign, x * half : (x + 1) * half, :] = high
                    low_ref[c, parity, sign, x * half : (x + 1) * half, :] = low


def gram_kernel(n_vec, n_grid, group, got_ref, high_ref, low_ref, out_ref):
    total = n_vec * group
    tile = 2 * group

    left, right = [], []
    for c in range(2):
        for parity in range(2):
            slabs = []
            for i in range(n_grid):
                start = (i * 2 + parity) * tile + c * group
                rows = [
                    got_ref[pl.ds(start + v, n_vec, stride=n_grid * 2 * tile), :]
                    for v in range(group)
                ]
                slabs.append(jnp.concatenate(rows, 0))
            for sign in range(2):
                folded = []
                for i in range(n_grid // 2):
                    near, far = slabs[i], slabs[n_grid - 1 - i]
                    folded.append(near - far if sign else near + far)
                value = jnp.concatenate(folded, 1)
                high, low = split_bf16(value)
                op_high, op_low = high_ref[c, parity, sign], low_ref[c, parity, sign]
                both = jnp.dot(
                    jnp.concatenate([high, low], 0), op_high, preferred_element_type=jnp.float32
                )
                applied = both[:total] + both[total:]
                applied += jnp.dot(high, op_low, preferred_element_type=jnp.float32)
                left.append(jnp.concatenate(split_bf16(applied), 0))
                right.append(jnp.concatenate([high, low], 0))
    gram = lax.dot_general(
        jnp.concatenate(left, 1),
        jnp.concatenate(right, 1),
        (((1,), (1,)), ((), ())),
        preferred_element_type=jnp.float32,
    )
    gram = gram[:total] + gram[total:]
    gram = jnp.concatenate([gram, jnp.zeros((total, LANES - 2 * total), jnp.float32)], 1)
    for v in range(group):
        out_ref[pl.ds(v, n_vec, stride=group), :] = gram[v * n_vec : (v + 1) * n_vec]


def finish_kernel(n_vec, got_ref, out_ref):
    _, group, shifts = out_ref.shape
    total = n_vec * group
    g = lax.axis_index("vec")
    summed = jnp.sum(got_ref[...], 0, keepdims=True)
    lane = lax.broadcasted_iota(jnp.int32, summed.shape, 1)

    def from_lane(first):
        return pltpu.roll(summed, lax.rem(2 * LANES - first, LANES), 1)

    for w in range(group):
        start = w * n_vec + g
        ahead = from_lane(start) + from_lane(start + total)
        behind = from_lane(start - n_vec) + from_lane(start - n_vec + total)
        out_ref[0, w : w + 1, :] = jnp.where(lane < n_vec - g, ahead, behind)[:, :shifts]


def whole_blocks(count):
    return [pl.BlockSpec(memory_space=pltpu.VMEM)] * count


def tiled_program(fitting_vectors, size, n_vec, n_grid, shifts):
    group, slab, _ = fitting_vectors.shape
    half = size // 2
    n_devices = n_vec * n_grid
    total = n_vec * group
    pair = lax.axis_index(AXES)

    spread = np.einsum("kcz,vw->kcvwz", pair_table(size), np.eye(group))
    high, low = split_table(spread.reshape(size * 2 * group, group * size))
    table = jnp.asarray(np.concatenate([high, low], 1))
    chunk_shape = (size, 2, 2 * group, LANES)
    components = pl.pallas_call(
        functools.partial(analyse_kernel, size, n_grid),
        out_shape=jax.ShapeDtypeStruct(chunk_shape, jnp.float32),
        in_specs=[pl.BlockSpec(memory_space=pltpu.HBM)] * 2,
        out_specs=pl.BlockSpec(memory_space=pltpu.HBM),
        scratch_shapes=[
            pltpu.VMEM(fitting_vectors.shape, jnp.float32),
            pltpu.VMEM(table.shape, table.dtype),
            pltpu.VMEM((2, half * slab, LANES), jnp.float32),
            pltpu.VMEM(chunk_shape, jnp.float32),
            pltpu.SemaphoreType.DMA((group + 1 + OUT_COPIES,)),
        ],
        compiler_params=ALL_VMEM,
        name="analyse",
    )(fitting_vectors, table)
    got = lax.all_to_all(components, AXES, 0, 0, tiled=True)

    omega = math.pi / size
    ky_pad = -(size + 1) % ROWS
    kx_pad = -(size + 1) % ROWS
    spectrum = operator_spectrum(size, pair, kx_pad, ky_pad)
    freqs_y = np.arange(size + 1 + ky_pad)
    freqs_x = np.arange(size + 1 + kx_pad)
    offsets = np.arange(-(size - 1), size + 1)
    cos_table = np.repeat(np.cos(omega * np.outer(freqs_x, offsets)), half, 1)
    angle = omega * np.outer(freqs_y, centred(size)[:half])
    waves = np.stack([np.cos(angle), np.sin(angle)])
    waves[0, size] = 0.0
    waves[1, 0] = 0.0
    op_shape = jax.ShapeDtypeStruct((2, 2, 2, half * half, half * half), jnp.bfloat16)
    op_high, op_low = pl.pallas_call(
        functools.partial(operator_kernel, size),
        out_shape=(op_shape, op_shape),
        in_specs=whole_blocks(4),
        out_specs=tuple(whole_blocks(2)),
        compiler_params=PARAMS,
        name="operator",
    )(
        spectrum,
        jnp.asarray(cos_table, jnp.float32),
        jnp.asarray(np.tile(waves, (1, 1, 2 * size)), jnp.float32),
        jnp.asarray(np.swapaxes(waves, 1, 2), jnp.float32),
    )

    rows = pl.pallas_call(
        functools.partial(gram_kernel, n_vec, n_grid, group),
        out_shape=jax.ShapeDtypeStruct((total, LANES), jnp.float32),
        in_specs=whole_blocks(3),
        out_specs=whole_blocks(1)[0],
        compiler_params=PARAMS,
        name="gram",
    )(got.reshape(n_devices * 4 * group, LANES), op_high, op_low)
    parts = lax.all_to_all(rows, AXES, 0, 0, tiled=True)
    return pl.pallas_call(
        functools.partial(finish_kernel, n_vec),
        out_shape=jax.ShapeDtypeStruct((1, group, shifts), jnp.float32),
        in_specs=whole_blocks(1),
        out_specs=whole_blocks(1)[0],
        compiler_params=PARAMS,
        name="finish",
    )(parts).transpose(0, 2, 1)


def general_program(fitting_vectors, size, n_vec, n_grid, shifts):
    exact = lax.Precision.HIGHEST
    group, slab, _ = fitting_vectors.shape
    n_devices = n_vec * n_grid
    total = n_vec * group
    rank = lax.axis_index(AXES)
    sharers = max(1, n_devices // size)
    held = max(1, size // n_devices)
    components = jnp.einsum(
        "vxyz,kcz->kcvxy",
        fitting_vectors.reshape(group, slab, size, size),
        jnp.asarray(pair_table(size)),
        precision=exact,
    )
    chunks = jnp.repeat(components, sharers, 0)
    chunks = chunks.reshape(n_devices, held, 2, group, slab, size)
    got = lax.all_to_all(chunks, AXES, 0, 0, tiled=True)
    got = got.reshape(n_vec, n_grid, held, 2, group, slab, size)
    planes = got.transpose(2, 3, 0, 4, 1, 5, 6).reshape(held, 2, total, size * size)

    omega = math.pi / size
    cells = np.arange(size)
    steps = np.cos(
        omega * (cells[:, None, None] - cells[None, :, None]) * np.arange(size + 1)
    ).astype(np.float32)
    columns = size * size // sharers
    start = rank % sharers * columns
    gram = jnp.zeros((total, total), jnp.float32)
    for h in range(held):
        spectrum = operator_spectrum(size, rank // sharers * held + h)
        along = jnp.einsum("clk,xak->clxa", spectrum, steps, precision=exact)
        operator = jnp.einsum("ybl,clxa->cxyab", steps, along, precision=exact)
        operator = operator.reshape(2, size * size, size * size)
        operator = lax.dynamic_slice_in_dim(operator, start, columns, 2)
        applied = jnp.einsum("cmp,cpq->cmq", planes[h], operator, precision=exact)
        own = lax.dynamic_slice_in_dim(planes[h], start, columns, 2)
        gram += jnp.einsum("cmq,cnq->mn", applied, own, precision=exact)
    wanted = (np.arange(n_vec)[:, None] * group + np.arange(shifts * group)) % total
    wanted = np.repeat(wanted, group, 0)
    rows = jnp.take_along_axis(gram, jnp.asarray(wanted), 1)
    rows = rows.reshape(n_devices, total // n_devices, shifts * group)
    parts = lax.all_to_all(rows, AXES, 0, 0, tiled=True)
    return jnp.sum(parts, 0).reshape(total // n_devices, shifts, group)


def body(fitting_vectors):
    n_vec, n_grid = (lax.axis_size(a) for a in AXES)
    group, slab, plane = fitting_vectors.shape
    size = math.isqrt(plane)
    shifts = n_vec // 2 + 1
    tiled = (
        n_vec * n_grid == size
        and group * size == LANES
        and slab * size == 2 * LANES
        and 2 * group == ROWS
        and n_vec * group <= LANES
        and n_vec % 2 == 0
        and n_grid % 2 == 0
        and group == n_grid
    )
    build = tiled_program if tiled else general_program
    return build(fitting_vectors, size, n_vec, n_grid, shifts)


def solution(mesh):
    return jax.shard_map(
        body,
        mesh=mesh,
        in_specs=(P("vec", "grid", None),),
        out_specs=P(("vec", "grid"), None, None),
        check_vma=False,
    )
```

```python
import functools
import math

import jax
import jax.numpy as jnp
import numpy as np
from jax import lax
from jax.experimental import pallas as pl
from jax.experimental.pallas import tpu as pltpu
from jax.sharding import PartitionSpec as P

AXES = ("vec", "grid")
LANES = 128
ROWS = 8
OUT_COPIES = 4
PARAMS = pltpu.CompilerParams(vmem_limit_bytes=16 * 2**20)
ALL_VMEM = pltpu.CompilerParams(vmem_limit_bytes=60 * 2**20)


def centred(size):
    return np.arange(size) - (size - 1) / 2


def pair_table(size):
    omega = math.pi / size
    freqs = np.arange(size)
    cosines = np.cos(omega * np.outer(freqs, centred(size)))
    sines = np.sin(omega * np.outer(np.where(freqs == 0, size, freqs), centred(size)))
    return np.stack([cosines, sines], 1).astype(np.float32)


def multiplicity(size):
    return np.where(np.isin(np.arange(size + 1), (0, size)), 1.0, 2.0)


def operator_spectrum(size, pair, kx_pad=0, ky_pad=0):
    kz = jnp.stack([pair, jnp.where(pair == 0, size, pair)]).astype(jnp.float32)
    times = jnp.where(pair == 0, 1.0, 2.0)
    ky = jnp.arange(size + 1 + ky_pad, dtype=jnp.int32)
    kx = jnp.arange(size + 1 + kx_pad, dtype=jnp.int32)
    fy, fx = ky.astype(jnp.float32), kx.astype(jnp.float32)
    total_sq = (kz * kz)[:, None, None] + (fy * fy)[None, :, None] + (fx * fx)[None, None, :]
    wave_sq = total_sq * (math.pi / size) ** 2
    safe_sq = jnp.where(total_sq > 0, wave_sq, 1.0)
    half_arg = 0.5 * jnp.sqrt(safe_sq) * size
    values = 8.0 * math.pi * jnp.sin(half_arg) ** 2 / safe_sq
    values = jnp.where(total_sq > 0, values, 2.0 * math.pi * size * size)

    def weight(k):
        inside = jnp.where((k == 0) | (k == size), 1.0, 2.0)
        return jnp.where(k <= size, inside, 0.0)

    scale = times / (float(2 * size) ** 3 * float(size) ** 3)
    return values * weight(ky)[None, :, None] * weight(kx)[None, None, :] * scale


def split_bf16(value):
    high = value.astype(jnp.bfloat16)
    return high, (value - high.astype(jnp.float32)).astype(jnp.bfloat16)


def split_table(table):
    table = np.asarray(table, np.float32)
    high = table.astype(jnp.bfloat16)
    return high, (table - high.astype(np.float32)).astype(jnp.bfloat16)


def analyse_kernel(
    size, n_grid, field_hbm, table_hbm, out_hbm, field_ref, table_ref, held_ref, out_ref, sems
):
    group, slab, _ = field_ref.shape
    half = size // 2
    per_block = LANES // size
    blocks = size // per_block
    field_copies = [
        pltpu.make_async_copy(field_hbm.at[v], field_ref.at[v], sems.at[v]) for v in range(group)
    ]
    table_copy = pltpu.make_async_copy(table_hbm, table_ref, sems.at[group])
    for copy in field_copies:
        copy.start()
    table_copy.start()
    mirrored = lax.axis_index("grid") >= n_grid // 2
    lane_group = lax.broadcasted_iota(jnp.int32, (blocks * slab, LANES), 1) // size
    for copy in field_copies:
        copy.wait()
    stacked = [
        jnp.concatenate([field_ref[v, :, b * LANES : (b + 1) * LANES] for b in range(blocks)], 0)
        for v in range(group)
    ]
    turned = []
    for q in range(per_block):
        mixed = None
        for v in range(group):
            shift = (v - q) % per_block * size
            part = pltpu.roll(stacked[v], shift, 1) if shift else stacked[v]
            mixed = part if mixed is None else jnp.where(lane_group == v, part, mixed)
        turned.append(mixed)
    for y in range(half):
        b, q = divmod(y, per_block)
        other_b, other_q = divmod(size - 1 - y, per_block)
        near = turned[q][b * slab : (b + 1) * slab]
        far = turned[other_q][other_b * slab : (other_b + 1) * slab]
        held_ref[0, y * slab : (y + 1) * slab, :] = near + far
        held_ref[1, y * slab : (y + 1) * slab, :] = near - far
    rows = []
    for parity in range(2):
        for j in range(slab):
            start = jnp.where(mirrored, slab - 1 - j, j)
            rows.append(held_ref[parity, pl.ds(start, half, stride=slab), :])
    high, low = split_bf16(jnp.concatenate(rows, 0))
    operand = jnp.concatenate([high, high, low], 1)
    table_copy.wait()
    table = jnp.concatenate([table_ref[...], table_ref[:, :LANES]], 1)
    values = lax.dot_general(
        table, operand, (((1,), (1,)), ((), ())), preferred_element_type=jnp.float32
    )
    parts = sems.shape[0] - group - 1
    step = size // parts
    out_copies = []
    for p in range(parts):
        rows = slice(p * step * 2 * group, (p + 1) * step * 2 * group)
        own = slice(p * step, (p + 1) * step)
        for parity in range(2):
            part = values[rows, parity * LANES : (parity + 1) * LANES]
            out_ref[own, parity] = part.reshape(step, 2 * group, LANES)
        copy = pltpu.make_async_copy(out_ref.at[own], out_hbm.at[own], sems.at[group + 1 + p])
        copy.start()
        out_copies.append(copy)
    for copy in out_copies:
        copy.wait()


def operator_kernel(size, spectrum_ref, cos_ref, wave_ref, turn_ref, high_ref, low_ref):
    half = size // 2
    width = half * half
    exact = lax.Precision.HIGHEST
    for c in range(2):
        along = jnp.dot(
            spectrum_ref[c], cos_ref[...], precision=exact, preferred_element_type=jnp.float32
        )
        for parity in range(2):
            strip = jnp.dot(
                turn_ref[parity],
                along * wave_ref[parity],
                precision=exact,
                preferred_element_type=jnp.float32,
            )

            def window(start):
                base = start // LANES * LANES
                part = strip[:, base : base + width + LANES]
                if start > base:
                    part = pltpu.roll(part, part.shape[1] - (start - base), 1)
                return part[:, :width]

            for x in range(half):
                toeplitz = window((size - 1 - x) * half)
                hankel = window(x * half)
                for sign in range(2):
                    value = 0.5 * (toeplitz - hankel if sign else toeplitz + hankel)
                    high, low = split_bf16(value)
                    high_ref[c, parity, sign, x * half : (x + 1) * half, :] = high
                    low_ref[c, parity, sign, x * half : (x + 1) * half, :] = low


def gram_kernel(n_vec, n_grid, group, got_ref, high_ref, low_ref, out_ref):
    total = n_vec * group
    tile = 2 * group

    def apply(high, low, which):
        op_high, op_low = high_ref[which], low_ref[which]
        both = jnp.dot(
            jnp.concatenate([high, low], 0), op_high, preferred_element_type=jnp.float32
        )
        applied = both[: high.shape[0]] + both[high.shape[0] :]
        return applied + jnp.dot(high, op_low, preferred_element_type=jnp.float32)

    def gram_rows(one_operator):
        left, right = [], []
        for parity in range(2):
            slabs = []
            for i in range(n_grid):
                start = (i * 2 + parity) * tile
                rows = [
                    got_ref[pl.ds(start + row, n_vec, stride=n_grid * 2 * tile), :]
                    for row in range(tile)
                ]
                slabs.append(jnp.concatenate(rows, 0))
            for sign in range(2):
                folded = []
                for i in range(n_grid // 2):
                    near, far = slabs[i], slabs[n_grid - 1 - i]
                    folded.append(near - far if sign else near + far)
                high, low = split_bf16(jnp.concatenate(folded, 1))
                own = [slice(c * total, (c + 1) * total) for c in range(2)]
                if one_operator:
                    applied = apply(high, low, (0, parity, sign))
                else:
                    applied = jnp.concatenate(
                        [apply(high[own[c]], low[own[c]], (c, parity, sign)) for c in range(2)], 0
                    )
                applied_high, applied_low = split_bf16(applied)
                for rows in own:
                    left.append(jnp.concatenate([applied_high[rows], applied_low[rows]], 0))
                    right.append(jnp.concatenate([high[rows], low[rows]], 0))
        gram = lax.dot_general(
            jnp.concatenate(left, 1),
            jnp.concatenate(right, 1),
            (((1,), (1,)), ((), ())),
            preferred_element_type=jnp.float32,
        )
        gram = gram[:total] + gram[total:]
        gram = jnp.concatenate([gram, jnp.zeros((total, LANES - 2 * total), jnp.float32)], 1)
        for v in range(group):
            out_ref[pl.ds(v, n_vec, stride=group), :] = gram[v * n_vec : (v + 1) * n_vec]

    first = (lax.axis_index("vec") == 0) & (lax.axis_index("grid") == 0)

    @pl.when(first)
    def _():
        gram_rows(False)

    @pl.when(jnp.logical_not(first))
    def _():
        gram_rows(True)


def finish_kernel(n_vec, got_ref, out_ref):
    _, group, shifts = out_ref.shape
    total = n_vec * group
    g = lax.axis_index("vec")
    summed = jnp.sum(got_ref[...], 0, keepdims=True)
    lane = lax.broadcasted_iota(jnp.int32, summed.shape, 1)

    def from_lane(first):
        return pltpu.roll(summed, lax.rem(2 * LANES - first, LANES), 1)

    for w in range(group):
        start = w * n_vec + g
        ahead = from_lane(start) + from_lane(start + total)
        behind = from_lane(start - n_vec) + from_lane(start - n_vec + total)
        out_ref[0, w : w + 1, :] = jnp.where(lane < n_vec - g, ahead, behind)[:, :shifts]


def whole_blocks(count):
    return [pl.BlockSpec(memory_space=pltpu.VMEM)] * count


def tiled_program(fitting_vectors, size, n_vec, n_grid, shifts):
    group, slab, _ = fitting_vectors.shape
    half = size // 2
    n_devices = n_vec * n_grid
    total = n_vec * group
    pair = lax.axis_index(AXES)

    spread = np.einsum("kcz,vw->kcvwz", pair_table(size), np.eye(group))
    high, low = split_table(spread.reshape(size * 2 * group, group * size))
    table = jnp.asarray(np.concatenate([high, low], 1))
    chunk_shape = (size, 2, 2 * group, LANES)
    components = pl.pallas_call(
        functools.partial(analyse_kernel, size, n_grid),
        out_shape=jax.ShapeDtypeStruct(chunk_shape, jnp.float32),
        in_specs=[pl.BlockSpec(memory_space=pltpu.HBM)] * 2,
        out_specs=pl.BlockSpec(memory_space=pltpu.HBM),
        scratch_shapes=[
            pltpu.VMEM(fitting_vectors.shape, jnp.float32),
            pltpu.VMEM(table.shape, table.dtype),
            pltpu.VMEM((2, half * slab, LANES), jnp.float32),
            pltpu.VMEM(chunk_shape, jnp.float32),
            pltpu.SemaphoreType.DMA((group + 1 + OUT_COPIES,)),
        ],
        compiler_params=ALL_VMEM,
        name="analyse",
    )(fitting_vectors, table)
    got = lax.all_to_all(components, AXES, 0, 0, tiled=True)

    omega = math.pi / size
    ky_pad = -(size + 1) % ROWS
    kx_pad = -(size + 1) % ROWS
    spectrum = operator_spectrum(size, pair, kx_pad, ky_pad)
    freqs_y = np.arange(size + 1 + ky_pad)
    freqs_x = np.arange(size + 1 + kx_pad)
    offsets = np.arange(-(size - 1), size + 1)
    cos_table = np.repeat(np.cos(omega * np.outer(freqs_x, offsets)), half, 1)
    angle = omega * np.outer(freqs_y, centred(size)[:half])
    waves = np.stack([np.cos(angle), np.sin(angle)])
    waves[0, size] = 0.0
    waves[1, 0] = 0.0
    op_shape = jax.ShapeDtypeStruct((2, 2, 2, half * half, half * half), jnp.bfloat16)
    op_high, op_low = pl.pallas_call(
        functools.partial(operator_kernel, size),
        out_shape=(op_shape, op_shape),
        in_specs=whole_blocks(4),
        out_specs=tuple(whole_blocks(2)),
        compiler_params=PARAMS,
        name="operator",
    )(
        spectrum,
        jnp.asarray(cos_table, jnp.float32),
        jnp.asarray(np.tile(waves, (1, 1, 2 * size)), jnp.float32),
        jnp.asarray(np.swapaxes(waves, 1, 2), jnp.float32),
    )

    rows = pl.pallas_call(
        functools.partial(gram_kernel, n_vec, n_grid, group),
        out_shape=jax.ShapeDtypeStruct((total, LANES), jnp.float32),
        in_specs=whole_blocks(3),
        out_specs=whole_blocks(1)[0],
        compiler_params=PARAMS,
        name="gram",
    )(got.reshape(n_devices * 4 * group, LANES), op_high, op_low)
    parts = lax.all_to_all(rows, AXES, 0, 0, tiled=True)
    return pl.pallas_call(
        functools.partial(finish_kernel, n_vec),
        out_shape=jax.ShapeDtypeStruct((1, group, shifts), jnp.float32),
        in_specs=whole_blocks(1),
        out_specs=whole_blocks(1)[0],
        compiler_params=PARAMS,
        name="finish",
    )(parts).transpose(0, 2, 1)


def general_program(fitting_vectors, size, n_vec, n_grid, shifts):
    exact = lax.Precision.HIGHEST
    group, slab, _ = fitting_vectors.shape
    n_devices = n_vec * n_grid
    total = n_vec * group
    rank = lax.axis_index(AXES)
    sharers = max(1, n_devices // size)
    held = max(1, size // n_devices)
    components = jnp.einsum(
        "vxyz,kcz->kcvxy",
        fitting_vectors.reshape(group, slab, size, size),
        jnp.asarray(pair_table(size)),
        precision=exact,
    )
    chunks = jnp.repeat(components, sharers, 0)
    chunks = chunks.reshape(n_devices, held, 2, group, slab, size)
    got = lax.all_to_all(chunks, AXES, 0, 0, tiled=True)
    got = got.reshape(n_vec, n_grid, held, 2, group, slab, size)
    planes = got.transpose(2, 3, 0, 4, 1, 5, 6).reshape(held, 2, total, size * size)

    omega = math.pi / size
    cells = np.arange(size)
    steps = np.cos(
        omega * (cells[:, None, None] - cells[None, :, None]) * np.arange(size + 1)
    ).astype(np.float32)
    columns = size * size // sharers
    start = rank % sharers * columns
    gram = jnp.zeros((total, total), jnp.float32)
    for h in range(held):
        spectrum = operator_spectrum(size, rank // sharers * held + h)
        along = jnp.einsum("clk,xak->clxa", spectrum, steps, precision=exact)
        operator = jnp.einsum("ybl,clxa->cxyab", steps, along, precision=exact)
        operator = operator.reshape(2, size * size, size * size)
        operator = lax.dynamic_slice_in_dim(operator, start, columns, 2)
        applied = jnp.einsum("cmp,cpq->cmq", planes[h], operator, precision=exact)
        own = lax.dynamic_slice_in_dim(planes[h], start, columns, 2)
        gram += jnp.einsum("cmq,cnq->mn", applied, own, precision=exact)
    wanted = (np.arange(n_vec)[:, None] * group + np.arange(shifts * group)) % total
    wanted = np.repeat(wanted, group, 0)
    rows = jnp.take_along_axis(gram, jnp.asarray(wanted), 1)
    rows = rows.reshape(n_devices, total // n_devices, shifts * group)
    parts = lax.all_to_all(rows, AXES, 0, 0, tiled=True)
    return jnp.sum(parts, 0).reshape(total // n_devices, shifts, group)


def body(fitting_vectors):
    n_vec, n_grid = (lax.axis_size(a) for a in AXES)
    group, slab, plane = fitting_vectors.shape
    size = math.isqrt(plane)
    shifts = n_vec // 2 + 1
    tiled = (
        n_vec * n_grid == size
        and group * size == LANES
        and slab * size == 2 * LANES
        and 2 * group == ROWS
        and n_vec * group <= LANES
        and n_vec % 2 == 0
        and n_grid % 2 == 0
        and group == n_grid
    )
    build = tiled_program if tiled else general_program
    return build(fitting_vectors, size, n_vec, n_grid, shifts)


def solution(mesh):
    return jax.shard_map(
        body,
        mesh=mesh,
        in_specs=(P("vec", "grid", None),),
        out_specs=P(("vec", "grid"), None, None),
        check_vma=False,
    )
```

```python
import functools
import math

import jax
import jax.numpy as jnp
import numpy as np
from jax import lax
from jax.experimental import pallas as pl
from jax.experimental.pallas import tpu as pltpu
from jax.sharding import PartitionSpec as P

AXES = ("vec", "grid")
LANES = 128
ROWS = 8
PARAMS = pltpu.CompilerParams(vmem_limit_bytes=16 * 2**20)


def centred(size):
    return np.arange(size) - (size - 1) / 2


def pair_table(size):
    omega = math.pi / size
    freqs = np.arange(size)
    cosines = np.cos(omega * np.outer(freqs, centred(size)))
    sines = np.sin(omega * np.outer(np.where(freqs == 0, size, freqs), centred(size)))
    return np.stack([cosines, sines], 1).astype(np.float32)


def multiplicity(size):
    return np.where(np.isin(np.arange(size + 1), (0, size)), 1.0, 2.0)


def kernel_values(size, kz, ky, kx):
    total_sq = kz * kz + ky * ky + kx * kx
    wave_sq = total_sq * (math.pi / size) ** 2
    safe_sq = jnp.where(total_sq > 0, wave_sq, 1.0)
    half_arg = 0.5 * jnp.sqrt(safe_sq) * size
    values = 8.0 * math.pi * jnp.sin(half_arg) ** 2 / safe_sq
    return jnp.where(total_sq > 0, values, 2.0 * math.pi * size * size)


def times(size, k):
    inside = jnp.where((k == 0) | (k == size), 1.0, 2.0)
    return jnp.where(k <= size, inside, 0.0)


def scaled(size, values, pair, ky, kx):
    scale = 1.0 / (float(2 * size) ** 3 * float(size) ** 3)
    return values * times(size, ky) * times(size, kx) * jnp.where(pair == 0, scale, 2.0 * scale)


def operator_spectrum(size, pair, c, n_ky):
    ky = lax.broadcasted_iota(jnp.int32, (n_ky, LANES), 0)
    kx = lax.broadcasted_iota(jnp.int32, (n_ky, LANES), 1)
    kz = jnp.where(pair == 0, size, pair) if c else pair
    fz, fy, fx = (k.astype(jnp.float32) for k in (kz, ky, kx))
    return scaled(size, kernel_values(size, fz, fy, fx), pair, ky, kx)


def pair_spectrum(size, pair):
    kz = jnp.stack([pair, jnp.where(pair == 0, size, pair)])[:, None, None]
    ky = jnp.arange(size + 1, dtype=jnp.int32)[None, :, None]
    kx = jnp.arange(size + 1, dtype=jnp.int32)[None, None, :]
    fz, fy, fx = (k.astype(jnp.float32) for k in (kz, ky, kx))
    return scaled(size, kernel_values(size, fz, fy, fx), pair, ky, kx)


def split_bf16(value):
    high = value.astype(jnp.bfloat16)
    return high, (value - high.astype(jnp.float32)).astype(jnp.bfloat16)


def split_table(table):
    table = np.asarray(table, np.float32)
    high = table.astype(jnp.bfloat16)
    return high, (table - high.astype(np.float32)).astype(jnp.bfloat16)


def prepare_kernel(
    size,
    n_grid,
    field_hbm,
    table_hbm,
    cos_hbm,
    wave_hbm,
    turn_hbm,
    out_ref,
    high_ref,
    low_ref,
    field_ref,
    table_ref,
    cos_ref,
    wave_ref,
    turn_ref,
    held_ref,
    sems,
):
    group, slab, _ = field_ref.shape
    half = size // 2
    per_block = LANES // size
    blocks = size // per_block
    field_copies = [
        pltpu.make_async_copy(field_hbm.at[v], field_ref.at[v], sems.at[v]) for v in range(group)
    ]
    pairs = ((table_hbm, table_ref), (cos_hbm, cos_ref), (wave_hbm, wave_ref), (turn_hbm, turn_ref))
    table_copies = [
        pltpu.make_async_copy(source, target, sems.at[group + t])
        for t, (source, target) in enumerate(pairs)
    ]
    for copy in field_copies + table_copies:
        copy.start()
    n_ky = wave_ref.shape[1]
    pair = lax.axis_index("vec") * n_grid + lax.axis_index("grid")
    spectrum = operator_spectrum(size, pair, 0, n_ky)
    mirrored = lax.axis_index("grid") >= n_grid // 2
    lane_group = lax.broadcasted_iota(jnp.int32, (blocks * slab, LANES), 1) // size
    for copy in field_copies:
        copy.wait()
    stacked = [
        jnp.concatenate([field_ref[v, :, b * LANES : (b + 1) * LANES] for b in range(blocks)], 0)
        for v in range(group)
    ]
    turned = []
    for q in range(per_block):
        mixed = None
        for v in range(group):
            shift = (v - q) % per_block * size
            part = pltpu.roll(stacked[v], shift, 1) if shift else stacked[v]
            mixed = part if mixed is None else jnp.where(lane_group == v, part, mixed)
        turned.append(mixed)
    for y in range(half):
        b, q = divmod(y, per_block)
        other_b, other_q = divmod(size - 1 - y, per_block)
        near = turned[q][b * slab : (b + 1) * slab]
        far = turned[other_q][other_b * slab : (other_b + 1) * slab]
        held_ref[0, y * slab : (y + 1) * slab, :] = near + far
        held_ref[1, y * slab : (y + 1) * slab, :] = near - far
    rows = []
    for parity in range(2):
        for j in range(slab):
            start = jnp.where(mirrored, slab - 1 - j, j)
            rows.append(held_ref[parity, pl.ds(start, half, stride=slab), :])
    high, low = split_bf16(jnp.concatenate(rows, 0))
    operand = jnp.concatenate([high, high, low], 1)
    for copy in table_copies:
        copy.wait()
    table = jnp.concatenate([table_ref[...], table_ref[:, :LANES]], 1)
    values = lax.dot_general(
        table, operand, (((1,), (1,)), ((), ())), preferred_element_type=jnp.float32
    )
    for parity in range(2):
        part = values[:, parity * LANES : (parity + 1) * LANES]
        out_ref[:, parity] = part.reshape(size, 2 * group, LANES)

    width = half * half
    exact = lax.Precision.HIGHEST
    spread = [jnp.concatenate([wave_ref[p]] * (cos_ref.shape[1] // LANES), 1) for p in range(2)]

    def build(c, spectrum):
        along = jnp.dot(
            spectrum[:, : cos_ref.shape[0]],
            cos_ref[...],
            precision=exact,
            preferred_element_type=jnp.float32,
        )
        strips = jnp.dot(
            turn_ref[...],
            jnp.concatenate([along * spread[p] for p in range(2)], 0),
            precision=exact,
            preferred_element_type=jnp.float32,
        )
        for parity in range(2):
            strip = strips[parity * half : (parity + 1) * half]

            def window(start):
                base = start // LANES * LANES
                part = strip[:, base : base + width + LANES]
                if start > base:
                    part = pltpu.roll(part, part.shape[1] - (start - base), 1)
                return part[:, :width]

            for x in range(half):
                toeplitz = window((size - 1 - x) * half)
                hankel = window(x * half)
                for sign in range(2):
                    value = 0.5 * (toeplitz - hankel if sign else toeplitz + hankel)
                    high, low = split_bf16(value)
                    high_ref[c, parity, sign, x * half : (x + 1) * half, :] = high
                    low_ref[c, parity, sign, x * half : (x + 1) * half, :] = low

    build(0, spectrum)

    @pl.when(pair == 0)
    def _():
        build(1, operator_spectrum(size, pair, 1, n_ky))


def gram_kernel(n_vec, n_grid, group, got_ref, high_ref, low_ref, out_ref):
    total = n_vec * group
    tile = 2 * group

    def apply(high, low, which):
        op_high, op_low = high_ref[which], low_ref[which]
        both = jnp.dot(
            jnp.concatenate([high, low], 0), op_high, preferred_element_type=jnp.float32
        )
        applied = both[: high.shape[0]] + both[high.shape[0] :]
        return applied + jnp.dot(high, op_low, preferred_element_type=jnp.float32)

    def gram_rows(one_operator):
        left, right = [], []
        for parity in range(2):
            slabs = []
            for i in range(n_grid):
                start = (i * 2 + parity) * tile
                rows = [
                    got_ref[pl.ds(start + row, n_vec, stride=n_grid * 2 * tile), :]
                    for row in range(tile)
                ]
                slabs.append(jnp.concatenate(rows, 0))
            for sign in range(2):
                folded = []
                for i in range(n_grid // 2):
                    near, far = slabs[i], slabs[n_grid - 1 - i]
                    folded.append(near - far if sign else near + far)
                high, low = split_bf16(jnp.concatenate(folded, 1))
                own = [slice(c * total, (c + 1) * total) for c in range(2)]
                if one_operator:
                    applied = apply(high, low, (0, parity, sign))
                else:
                    applied = jnp.concatenate(
                        [apply(high[own[c]], low[own[c]], (c, parity, sign)) for c in range(2)], 0
                    )
                applied_high, applied_low = split_bf16(applied)
                for rows in own:
                    left.append(jnp.concatenate([applied_high[rows], applied_low[rows]], 0))
                    right.append(jnp.concatenate([high[rows], low[rows]], 0))
        gram = lax.dot_general(
            jnp.concatenate(left, 1),
            jnp.concatenate(right, 1),
            (((1,), (1,)), ((), ())),
            preferred_element_type=jnp.float32,
        )
        gram = gram[:total] + gram[total:]
        gram = jnp.concatenate([gram, jnp.zeros((total, LANES - 2 * total), jnp.float32)], 1)
        for v in range(group):
            out_ref[pl.ds(v, n_vec, stride=group), :] = gram[v * n_vec : (v + 1) * n_vec]

    first = (lax.axis_index("vec") == 0) & (lax.axis_index("grid") == 0)

    @pl.when(first)
    def _():
        gram_rows(False)

    @pl.when(jnp.logical_not(first))
    def _():
        gram_rows(True)


def finish_kernel(n_vec, got_ref, out_ref):
    _, group, shifts = out_ref.shape
    total = n_vec * group
    g = lax.axis_index("vec")
    summed = jnp.sum(got_ref[...], 0, keepdims=True)
    lane = lax.broadcasted_iota(jnp.int32, summed.shape, 1)

    def from_lane(first):
        return pltpu.roll(summed, lax.rem(2 * LANES - first, LANES), 1)

    for w in range(group):
        start = w * n_vec + g
        ahead = from_lane(start) + from_lane(start + total)
        behind = from_lane(start - n_vec) + from_lane(start - n_vec + total)
        out_ref[0, w : w + 1, :] = jnp.where(lane < n_vec - g, ahead, behind)[:, :shifts]


def whole_blocks(count):
    return [pl.BlockSpec(memory_space=pltpu.VMEM)] * count


def tiled_program(fitting_vectors, size, n_vec, n_grid, shifts):
    group, slab, _ = fitting_vectors.shape
    half = size // 2
    n_devices = n_vec * n_grid
    total = n_vec * group
    spread = np.einsum("kcz,vw->kcvwz", pair_table(size), np.eye(group))
    high, low = split_table(spread.reshape(size * 2 * group, group * size))
    omega = math.pi / size
    freqs = np.arange(-(-(size + 1) // ROWS) * ROWS)
    offsets = np.arange(-(size - 1), size + 1)
    angle = omega * np.outer(freqs, centred(size)[:half])
    waves = np.stack([np.cos(angle), np.sin(angle)])
    waves[0, size] = 0.0
    waves[1, 0] = 0.0
    turn = np.einsum("pky,pq->pyqk", waves, np.eye(2))
    tables = [
        np.concatenate([high, low], 1),
        np.repeat(np.cos(omega * np.outer(freqs, offsets)), half, 1).astype(np.float32),
        np.tile(waves, (1, 1, LANES // half)).astype(np.float32),
        turn.reshape(2 * half, 2 * len(freqs)).astype(np.float32),
    ]
    op_shape = jax.ShapeDtypeStruct((2, 2, 2, half * half, half * half), jnp.bfloat16)
    arguments = [fitting_vectors] + [jnp.asarray(t) for t in tables]
    components, op_high, op_low = pl.pallas_call(
        functools.partial(prepare_kernel, size, n_grid),
        out_shape=(
            jax.ShapeDtypeStruct((size, 2, 2 * group, LANES), jnp.float32),
            op_shape,
            op_shape,
        ),
        in_specs=[pl.BlockSpec(memory_space=pltpu.HBM)] * len(arguments),
        out_specs=tuple(whole_blocks(3)),
        scratch_shapes=[pltpu.VMEM(a.shape, a.dtype) for a in arguments]
        + [
            pltpu.VMEM((2, half * slab, LANES), jnp.float32),
            pltpu.SemaphoreType.DMA((group + len(tables),)),
        ],
        compiler_params=PARAMS,
        name="prepare",
    )(*(pltpu.with_memory_space_constraint(a, pltpu.HBM) for a in arguments))
    got = lax.all_to_all(components, AXES, 0, 0, tiled=True)
    rows = pl.pallas_call(
        functools.partial(gram_kernel, n_vec, n_grid, group),
        out_shape=jax.ShapeDtypeStruct((total, LANES), jnp.float32),
        in_specs=whole_blocks(3),
        out_specs=whole_blocks(1)[0],
        compiler_params=PARAMS,
        name="gram",
    )(got.reshape(n_devices * 4 * group, LANES), op_high, op_low)
    parts = lax.all_to_all(rows, AXES, 0, 0, tiled=True)
    return pl.pallas_call(
        functools.partial(finish_kernel, n_vec),
        out_shape=jax.ShapeDtypeStruct((1, group, shifts), jnp.float32),
        in_specs=whole_blocks(1),
        out_specs=whole_blocks(1)[0],
        compiler_params=PARAMS,
        name="finish",
    )(parts).transpose(0, 2, 1)


def general_program(fitting_vectors, size, n_vec, n_grid, shifts):
    exact = lax.Precision.HIGHEST
    group, slab, _ = fitting_vectors.shape
    n_devices = n_vec * n_grid
    total = n_vec * group
    rank = lax.axis_index(AXES)
    sharers = max(1, n_devices // size)
    held = max(1, size // n_devices)
    components = jnp.einsum(
        "vxyz,kcz->kcvxy",
        fitting_vectors.reshape(group, slab, size, size),
        jnp.asarray(pair_table(size)),
        precision=exact,
    )
    chunks = jnp.repeat(components, sharers, 0)
    chunks = chunks.reshape(n_devices, held, 2, group, slab, size)
    got = lax.all_to_all(chunks, AXES, 0, 0, tiled=True)
    got = got.reshape(n_vec, n_grid, held, 2, group, slab, size)
    planes = got.transpose(2, 3, 0, 4, 1, 5, 6).reshape(held, 2, total, size * size)

    omega = math.pi / size
    cells = np.arange(size)
    steps = np.cos(
        omega * (cells[:, None, None] - cells[None, :, None]) * np.arange(size + 1)
    ).astype(np.float32)
    columns = size * size // sharers
    start = rank % sharers * columns
    gram = jnp.zeros((total, total), jnp.float32)
    for h in range(held):
        spectrum = pair_spectrum(size, rank // sharers * held + h)
        along = jnp.einsum("clk,xak->clxa", spectrum, steps, precision=exact)
        operator = jnp.einsum("ybl,clxa->cxyab", steps, along, precision=exact)
        operator = operator.reshape(2, size * size, size * size)
        operator = lax.dynamic_slice_in_dim(operator, start, columns, 2)
        applied = jnp.einsum("cmp,cpq->cmq", planes[h], operator, precision=exact)
        own = lax.dynamic_slice_in_dim(planes[h], start, columns, 2)
        gram += jnp.einsum("cmq,cnq->mn", applied, own, precision=exact)
    wanted = (np.arange(n_vec)[:, None] * group + np.arange(shifts * group)) % total
    wanted = np.repeat(wanted, group, 0)
    rows = jnp.take_along_axis(gram, jnp.asarray(wanted), 1)
    rows = rows.reshape(n_devices, total // n_devices, shifts * group)
    parts = lax.all_to_all(rows, AXES, 0, 0, tiled=True)
    return jnp.sum(parts, 0).reshape(total // n_devices, shifts, group)


def body(fitting_vectors):
    n_vec, n_grid = (lax.axis_size(a) for a in AXES)
    group, slab, plane = fitting_vectors.shape
    size = math.isqrt(plane)
    shifts = n_vec // 2 + 1
    tiled = (
        n_vec * n_grid == size
        and group * size == LANES
        and slab * size == 2 * LANES
        and 2 * group == ROWS
        and n_vec * group <= LANES
        and n_vec % 2 == 0
        and n_grid % 2 == 0
        and group == n_grid
    )
    build = tiled_program if tiled else general_program
    return build(fitting_vectors, size, n_vec, n_grid, shifts)


def solution(mesh):
    return jax.shard_map(
        body,
        mesh=mesh,
        in_specs=(P("vec", "grid", None),),
        out_specs=P(("vec", "grid"), None, None),
        check_vma=False,
    )
```

```python
import functools
import math

import jax
import jax.numpy as jnp
import numpy as np
from jax import lax
from jax.experimental import pallas as pl
from jax.experimental.pallas import tpu as pltpu
from jax.sharding import PartitionSpec as P

AXES = ("vec", "grid")
LANES = 128
ROWS = 8
PARAMS = pltpu.CompilerParams(vmem_limit_bytes=16 * 2**20)


def centred(size):
    return np.arange(size) - (size - 1) / 2


def pair_table(size):
    omega = math.pi / size
    freqs = np.arange(size)
    cosines = np.cos(omega * np.outer(freqs, centred(size)))
    sines = np.sin(omega * np.outer(np.where(freqs == 0, size, freqs), centred(size)))
    return np.stack([cosines, sines], 1).astype(np.float32)


def multiplicity(size):
    return np.where(np.isin(np.arange(size + 1), (0, size)), 1.0, 2.0)


def kernel_values(size, kz, ky, kx):
    total_sq = kz * kz + ky * ky + kx * kx
    wave_sq = total_sq * (math.pi / size) ** 2
    safe_sq = jnp.where(total_sq > 0, wave_sq, 1.0)
    half_arg = 0.5 * jnp.sqrt(safe_sq) * size
    values = 8.0 * math.pi * jnp.sin(half_arg) ** 2 / safe_sq
    return jnp.where(total_sq > 0, values, 2.0 * math.pi * size * size)


def times(size, k):
    inside = jnp.where((k == 0) | (k == size), 1.0, 2.0)
    return jnp.where(k <= size, inside, 0.0)


def scaled(size, values, pair, ky, kx):
    scale = 1.0 / (float(2 * size) ** 3 * float(size) ** 3)
    return values * times(size, ky) * times(size, kx) * jnp.where(pair == 0, scale, 2.0 * scale)


def operator_spectrum(size, pair, c, n_ky):
    ky = lax.broadcasted_iota(jnp.int32, (n_ky, LANES), 0)
    kx = lax.broadcasted_iota(jnp.int32, (n_ky, LANES), 1)
    kz = jnp.where(pair == 0, size, pair) if c else pair
    fz, fy, fx = (k.astype(jnp.float32) for k in (kz, ky, kx))
    return scaled(size, kernel_values(size, fz, fy, fx), pair, ky, kx)


def pair_spectrum(size, pair):
    kz = jnp.stack([pair, jnp.where(pair == 0, size, pair)])[:, None, None]
    ky = jnp.arange(size + 1, dtype=jnp.int32)[None, :, None]
    kx = jnp.arange(size + 1, dtype=jnp.int32)[None, None, :]
    fz, fy, fx = (k.astype(jnp.float32) for k in (kz, ky, kx))
    return scaled(size, kernel_values(size, fz, fy, fx), pair, ky, kx)


def split_bf16(value):
    high = value.astype(jnp.bfloat16)
    return high, (value - high.astype(jnp.float32)).astype(jnp.bfloat16)


def split_table(table):
    table = np.asarray(table, np.float32)
    high = table.astype(jnp.bfloat16)
    return high, (table - high.astype(np.float32)).astype(jnp.bfloat16)


def prepare_kernel(
    size,
    n_grid,
    field_hbm,
    table_hbm,
    cos_hbm,
    wave_hbm,
    turn_hbm,
    out_ref,
    high_ref,
    low_ref,
    field_ref,
    table_ref,
    cos_ref,
    wave_ref,
    turn_ref,
    held_ref,
    sems,
):
    group, slab, _ = field_ref.shape
    half = size // 2
    per_block = LANES // size
    blocks = size // per_block
    field_copies = [
        pltpu.make_async_copy(field_hbm.at[v], field_ref.at[v], sems.at[v]) for v in range(group)
    ]
    pairs = ((table_hbm, table_ref), (cos_hbm, cos_ref), (wave_hbm, wave_ref), (turn_hbm, turn_ref))
    table_copies = [
        pltpu.make_async_copy(source, target, sems.at[group + t])
        for t, (source, target) in enumerate(pairs)
    ]
    for copy in field_copies + table_copies:
        copy.start()
    n_ky = wave_ref.shape[1]
    pair = lax.axis_index("vec") * n_grid + lax.axis_index("grid")
    spectrum = operator_spectrum(size, pair, 0, n_ky)
    mirrored = lax.axis_index("grid") >= n_grid // 2
    lane_group = lax.broadcasted_iota(jnp.int32, (blocks * slab, LANES), 1) // size
    for copy in field_copies:
        copy.wait()
    stacked = [
        jnp.concatenate([field_ref[v, :, b * LANES : (b + 1) * LANES] for b in range(blocks)], 0)
        for v in range(group)
    ]
    turned = []
    for q in range(per_block):
        mixed = None
        for v in range(group):
            shift = (v - q) % per_block * size
            part = pltpu.roll(stacked[v], shift, 1) if shift else stacked[v]
            mixed = part if mixed is None else jnp.where(lane_group == v, part, mixed)
        turned.append(mixed)
    for y in range(half):
        b, q = divmod(y, per_block)
        other_b, other_q = divmod(size - 1 - y, per_block)
        near = turned[q][b * slab : (b + 1) * slab]
        far = turned[other_q][other_b * slab : (other_b + 1) * slab]
        held_ref[0, y * slab : (y + 1) * slab, :] = near + far
        held_ref[1, y * slab : (y + 1) * slab, :] = near - far
    rows = []
    for parity in range(2):
        for j in range(slab):
            start = jnp.where(mirrored, slab - 1 - j, j)
            rows.append(held_ref[parity, pl.ds(start, half, stride=slab), :])
    high, low = split_bf16(jnp.concatenate(rows, 0))
    operand = jnp.concatenate([high, high, low], 1)
    for copy in table_copies:
        copy.wait()
    width = half * half
    exact = lax.Precision.HIGHEST
    spread = [jnp.concatenate([wave_ref[p]] * (cos_ref.shape[1] // LANES), 1) for p in range(2)]

    def build(c, spectrum):
        along = jnp.dot(
            spectrum[:, : cos_ref.shape[0]],
            cos_ref[...],
            precision=exact,
            preferred_element_type=jnp.float32,
        )
        strips = jnp.dot(
            turn_ref[...],
            jnp.concatenate([along * spread[p] for p in range(2)], 0),
            precision=exact,
            preferred_element_type=jnp.float32,
        )
        for parity in range(2):
            strip = strips[parity * half : (parity + 1) * half]

            lanes = strip.shape[1]
            turned = [
                pltpu.roll(strip, lanes - shift, 1) if shift else strip
                for shift in range(0, LANES, half)
            ]

            def window(start):
                base = start // LANES * LANES
                return turned[(start - base) // half][:, base : base + width]

            for x in range(half):
                toeplitz = window((size - 1 - x) * half)
                hankel = window(x * half)
                for sign in range(2):
                    value = 0.5 * (toeplitz - hankel if sign else toeplitz + hankel)
                    high, low = split_bf16(value)
                    high_ref[c, parity, sign, x * half : (x + 1) * half, :] = high
                    low_ref[c, parity, sign, x * half : (x + 1) * half, :] = low

    build(0, spectrum)

    table = jnp.concatenate([table_ref[...], table_ref[:, :LANES]], 1)
    values = lax.dot_general(
        table, operand, (((1,), (1,)), ((), ())), preferred_element_type=jnp.float32
    )
    for parity in range(2):
        part = values[:, parity * LANES : (parity + 1) * LANES]
        out_ref[:, parity] = part.reshape(size, 2 * group, LANES)

    @pl.when(pair == 0)
    def _():
        build(1, operator_spectrum(size, pair, 1, n_ky))


def gram_kernel(n_vec, n_grid, group, got_ref, high_ref, low_ref, out_ref):
    total = n_vec * group
    tile = 2 * group

    def apply(high, low, which):
        op_high, op_low = high_ref[which], low_ref[which]
        both = jnp.dot(
            jnp.concatenate([high, low], 0), op_high, preferred_element_type=jnp.float32
        )
        applied = both[: high.shape[0]] + both[high.shape[0] :]
        return applied + jnp.dot(high, op_low, preferred_element_type=jnp.float32)

    def gram_rows(one_operator):
        left, right = [], []
        for parity in range(2):
            slabs = []
            for i in range(n_grid):
                start = (i * 2 + parity) * tile
                rows = [
                    got_ref[pl.ds(start + row, n_vec, stride=n_grid * 2 * tile), :]
                    for row in range(tile)
                ]
                slabs.append(jnp.concatenate(rows, 0))
            for sign in range(2):
                folded = []
                for i in range(n_grid // 2):
                    near, far = slabs[i], slabs[n_grid - 1 - i]
                    folded.append(near - far if sign else near + far)
                high, low = split_bf16(jnp.concatenate(folded, 1))
                own = [slice(c * total, (c + 1) * total) for c in range(2)]
                if one_operator:
                    applied = apply(high, low, (0, parity, sign))
                else:
                    applied = jnp.concatenate(
                        [apply(high[own[c]], low[own[c]], (c, parity, sign)) for c in range(2)], 0
                    )
                applied_high, applied_low = split_bf16(applied)
                for rows in own:
                    left.append(jnp.concatenate([applied_high[rows], applied_low[rows]], 0))
                    right.append(jnp.concatenate([high[rows], low[rows]], 0))
        gram = lax.dot_general(
            jnp.concatenate(left, 1),
            jnp.concatenate(right, 1),
            (((1,), (1,)), ((), ())),
            preferred_element_type=jnp.float32,
        )
        gram = gram[:total] + gram[total:]
        gram = jnp.concatenate([gram, jnp.zeros((total, LANES - 2 * total), jnp.float32)], 1)
        for v in range(group):
            out_ref[pl.ds(v, n_vec, stride=group), :] = gram[v * n_vec : (v + 1) * n_vec]

    first = (lax.axis_index("vec") == 0) & (lax.axis_index("grid") == 0)

    @pl.when(first)
    def _():
        gram_rows(False)

    @pl.when(jnp.logical_not(first))
    def _():
        gram_rows(True)


def finish_kernel(n_vec, got_ref, out_ref):
    _, group, shifts = out_ref.shape
    total = n_vec * group
    g = lax.axis_index("vec")
    summed = jnp.sum(got_ref[...], 0, keepdims=True)
    lane = lax.broadcasted_iota(jnp.int32, summed.shape, 1)

    def from_lane(first):
        return pltpu.roll(summed, lax.rem(2 * LANES - first, LANES), 1)

    for w in range(group):
        start = w * n_vec + g
        ahead = from_lane(start) + from_lane(start + total)
        behind = from_lane(start - n_vec) + from_lane(start - n_vec + total)
        out_ref[0, w : w + 1, :] = jnp.where(lane < n_vec - g, ahead, behind)[:, :shifts]


def whole_blocks(count):
    return [pl.BlockSpec(memory_space=pltpu.VMEM)] * count


def tiled_program(fitting_vectors, size, n_vec, n_grid, shifts):
    group, slab, _ = fitting_vectors.shape
    half = size // 2
    n_devices = n_vec * n_grid
    total = n_vec * group
    spread = np.einsum("kcz,vw->kcvwz", pair_table(size), np.eye(group))
    high, low = split_table(spread.reshape(size * 2 * group, group * size))
    omega = math.pi / size
    freqs = np.arange(-(-(size + 1) // ROWS) * ROWS)
    offsets = np.arange(-(size - 1), half + 1)
    angle = omega * np.outer(freqs, centred(size)[:half])
    waves = np.stack([np.cos(angle), np.sin(angle)])
    waves[0, size] = 0.0
    waves[1, 0] = 0.0
    turn = np.einsum("pky,pq->pyqk", waves, np.eye(2))
    tables = [
        np.concatenate([high, low], 1),
        np.repeat(np.cos(omega * np.outer(freqs, offsets)), half, 1).astype(np.float32),
        np.tile(waves, (1, 1, LANES // half)).astype(np.float32),
        turn.reshape(2 * half, 2 * len(freqs)).astype(np.float32),
    ]
    op_shape = jax.ShapeDtypeStruct((2, 2, 2, half * half, half * half), jnp.bfloat16)
    arguments = [fitting_vectors] + [jnp.asarray(t) for t in tables]
    components, op_high, op_low = pl.pallas_call(
        functools.partial(prepare_kernel, size, n_grid),
        out_shape=(
            jax.ShapeDtypeStruct((size, 2, 2 * group, LANES), jnp.float32),
            op_shape,
            op_shape,
        ),
        in_specs=[pl.BlockSpec(memory_space=pltpu.HBM)] * len(arguments),
        out_specs=tuple(whole_blocks(3)),
        scratch_shapes=[pltpu.VMEM(a.shape, a.dtype) for a in arguments]
        + [
            pltpu.VMEM((2, half * slab, LANES), jnp.float32),
            pltpu.SemaphoreType.DMA((group + len(tables),)),
        ],
        compiler_params=PARAMS,
        name="prepare",
    )(*(pltpu.with_memory_space_constraint(a, pltpu.HBM) for a in arguments))
    got = lax.all_to_all(components, AXES, 0, 0, tiled=True)
    rows = pl.pallas_call(
        functools.partial(gram_kernel, n_vec, n_grid, group),
        out_shape=jax.ShapeDtypeStruct((total, LANES), jnp.float32),
        in_specs=whole_blocks(3),
        out_specs=whole_blocks(1)[0],
        compiler_params=PARAMS,
        name="gram",
    )(got.reshape(n_devices * 4 * group, LANES), op_high, op_low)
    parts = lax.all_to_all(rows, AXES, 0, 0, tiled=True)
    return pl.pallas_call(
        functools.partial(finish_kernel, n_vec),
        out_shape=jax.ShapeDtypeStruct((1, group, shifts), jnp.float32),
        in_specs=whole_blocks(1),
        out_specs=whole_blocks(1)[0],
        compiler_params=PARAMS,
        name="finish",
    )(parts).transpose(0, 2, 1)


def general_program(fitting_vectors, size, n_vec, n_grid, shifts):
    exact = lax.Precision.HIGHEST
    group, slab, _ = fitting_vectors.shape
    n_devices = n_vec * n_grid
    total = n_vec * group
    rank = lax.axis_index(AXES)
    sharers = max(1, n_devices // size)
    held = max(1, size // n_devices)
    components = jnp.einsum(
        "vxyz,kcz->kcvxy",
        fitting_vectors.reshape(group, slab, size, size),
        jnp.asarray(pair_table(size)),
        precision=exact,
    )
    chunks = jnp.repeat(components, sharers, 0)
    chunks = chunks.reshape(n_devices, held, 2, group, slab, size)
    got = lax.all_to_all(chunks, AXES, 0, 0, tiled=True)
    got = got.reshape(n_vec, n_grid, held, 2, group, slab, size)
    planes = got.transpose(2, 3, 0, 4, 1, 5, 6).reshape(held, 2, total, size * size)

    omega = math.pi / size
    cells = np.arange(size)
    steps = np.cos(
        omega * (cells[:, None, None] - cells[None, :, None]) * np.arange(size + 1)
    ).astype(np.float32)
    columns = size * size // sharers
    start = rank % sharers * columns
    gram = jnp.zeros((total, total), jnp.float32)
    for h in range(held):
        spectrum = pair_spectrum(size, rank // sharers * held + h)
        along = jnp.einsum("clk,xak->clxa", spectrum, steps, precision=exact)
        operator = jnp.einsum("ybl,clxa->cxyab", steps, along, precision=exact)
        operator = operator.reshape(2, size * size, size * size)
        operator = lax.dynamic_slice_in_dim(operator, start, columns, 2)
        applied = jnp.einsum("cmp,cpq->cmq", planes[h], operator, precision=exact)
        own = lax.dynamic_slice_in_dim(planes[h], start, columns, 2)
        gram += jnp.einsum("cmq,cnq->mn", applied, own, precision=exact)
    wanted = (np.arange(n_vec)[:, None] * group + np.arange(shifts * group)) % total
    wanted = np.repeat(wanted, group, 0)
    rows = jnp.take_along_axis(gram, jnp.asarray(wanted), 1)
    rows = rows.reshape(n_devices, total // n_devices, shifts * group)
    parts = lax.all_to_all(rows, AXES, 0, 0, tiled=True)
    return jnp.sum(parts, 0).reshape(total // n_devices, shifts, group)


def body(fitting_vectors):
    n_vec, n_grid = (lax.axis_size(a) for a in AXES)
    group, slab, plane = fitting_vectors.shape
    size = math.isqrt(plane)
    shifts = n_vec // 2 + 1
    tiled = (
        n_vec * n_grid == size
        and group * size == LANES
        and slab * size == 2 * LANES
        and 2 * group == ROWS
        and n_vec * group <= LANES
        and n_vec % 2 == 0
        and n_grid % 2 == 0
        and group == n_grid
    )
    build = tiled_program if tiled else general_program
    return build(fitting_vectors, size, n_vec, n_grid, shifts)


def solution(mesh):
    return jax.shard_map(
        body,
        mesh=mesh,
        in_specs=(P("vec", "grid", None),),
        out_specs=P(("vec", "grid"), None, None),
        check_vma=False,
    )
```

```python
import functools
import math

import jax
import jax.numpy as jnp
import numpy as np
from jax import lax
from jax.experimental import pallas as pl
from jax.experimental.pallas import tpu as pltpu
from jax.sharding import PartitionSpec as P

AXES = ("vec", "grid")
LANES = 128
ROWS = 8
PARAMS = pltpu.CompilerParams(vmem_limit_bytes=16 * 2**20)


def centred(size):
    return np.arange(size) - (size - 1) / 2


def pair_table(size):
    omega = math.pi / size
    freqs = np.arange(size)
    cosines = np.cos(omega * np.outer(freqs, centred(size)))
    sines = np.sin(omega * np.outer(np.where(freqs == 0, size, freqs), centred(size)))
    return np.stack([cosines, sines], 1).astype(np.float32)


def multiplicity(size):
    return np.where(np.isin(np.arange(size + 1), (0, size)), 1.0, 2.0)


def kernel_values(size, kz, ky, kx):
    total_sq = kz * kz + ky * ky + kx * kx
    wave_sq = total_sq * (math.pi / size) ** 2
    safe_sq = jnp.where(total_sq > 0, wave_sq, 1.0)
    half_arg = 0.5 * jnp.sqrt(safe_sq) * size
    values = 8.0 * math.pi * jnp.sin(half_arg) ** 2 / safe_sq
    return jnp.where(total_sq > 0, values, 2.0 * math.pi * size * size)


def times(size, k):
    inside = jnp.where((k == 0) | (k == size), 1.0, 2.0)
    return jnp.where(k <= size, inside, 0.0)


def scaled(size, values, pair, ky, kx):
    scale = 1.0 / (float(2 * size) ** 3 * float(size) ** 3)
    return values * times(size, ky) * times(size, kx) * jnp.where(pair == 0, scale, 2.0 * scale)


def operator_spectrum(size, pair, c, n_ky):
    ky = lax.broadcasted_iota(jnp.int32, (n_ky, LANES), 0)
    kx = lax.broadcasted_iota(jnp.int32, (n_ky, LANES), 1)
    kz = jnp.where(pair == 0, size, pair) if c else pair
    fz, fy, fx = (k.astype(jnp.float32) for k in (kz, ky, kx))
    return scaled(size, kernel_values(size, fz, fy, fx), pair, ky, kx)


def pair_spectrum(size, pair):
    kz = jnp.stack([pair, jnp.where(pair == 0, size, pair)])[:, None, None]
    ky = jnp.arange(size + 1, dtype=jnp.int32)[None, :, None]
    kx = jnp.arange(size + 1, dtype=jnp.int32)[None, None, :]
    fz, fy, fx = (k.astype(jnp.float32) for k in (kz, ky, kx))
    return scaled(size, kernel_values(size, fz, fy, fx), pair, ky, kx)


def split_bf16(value):
    high = value.astype(jnp.bfloat16)
    return high, (value - high.astype(jnp.float32)).astype(jnp.bfloat16)


def split_table(table):
    table = np.asarray(table, np.float32)
    high = table.astype(jnp.bfloat16)
    return high, (table - high.astype(np.float32)).astype(jnp.bfloat16)


def prepare_kernel(
    size,
    n_grid,
    field_hbm,
    table_hbm,
    cos_hbm,
    wave_hbm,
    turn_hbm,
    out_ref,
    high_ref,
    low_ref,
    field_ref,
    table_ref,
    cos_ref,
    wave_ref,
    turn_ref,
    held_ref,
    sems,
):
    group, slab, _ = field_ref.shape
    half = size // 2
    per_block = LANES // size
    blocks = size // per_block
    field_copies = [
        pltpu.make_async_copy(field_hbm.at[v], field_ref.at[v], sems.at[v]) for v in range(group)
    ]
    pairs = ((table_hbm, table_ref), (cos_hbm, cos_ref), (wave_hbm, wave_ref), (turn_hbm, turn_ref))
    table_copies = [
        pltpu.make_async_copy(source, target, sems.at[group + t])
        for t, (source, target) in enumerate(pairs)
    ]
    for copy in field_copies + table_copies:
        copy.start()
    n_ky = wave_ref.shape[1]
    pair = lax.axis_index("vec") * n_grid + lax.axis_index("grid")
    spectrum = operator_spectrum(size, pair, 0, n_ky)
    mirrored = lax.axis_index("grid") >= n_grid // 2
    lane_group = lax.broadcasted_iota(jnp.int32, (blocks * slab, LANES), 1) // size
    for copy in field_copies:
        copy.wait()
    stacked = [
        jnp.concatenate([field_ref[v, :, b * LANES : (b + 1) * LANES] for b in range(blocks)], 0)
        for v in range(group)
    ]
    turned = []
    for q in range(per_block):
        mixed = None
        for v in range(group):
            shift = (v - q) % per_block * size
            part = pltpu.roll(stacked[v], shift, 1) if shift else stacked[v]
            mixed = part if mixed is None else jnp.where(lane_group == v, part, mixed)
        turned.append(mixed)
    for y in range(half):
        b, q = divmod(y, per_block)
        other_b, other_q = divmod(size - 1 - y, per_block)
        near = turned[q][b * slab : (b + 1) * slab]
        far = turned[other_q][other_b * slab : (other_b + 1) * slab]
        held_ref[0, y * slab : (y + 1) * slab, :] = near + far
        held_ref[1, y * slab : (y + 1) * slab, :] = near - far
    rows = []
    for parity in range(2):
        for j in range(slab):
            start = jnp.where(mirrored, slab - 1 - j, j)
            rows.append(held_ref[parity, pl.ds(start, half, stride=slab), :])
    high, low = split_bf16(jnp.concatenate(rows, 0))
    operand = jnp.concatenate([high, high, low], 1)
    for copy in table_copies:
        copy.wait()
    width = half * half
    exact = lax.Precision.HIGHEST
    spread = [jnp.concatenate([wave_ref[p]] * (cos_ref.shape[1] // LANES), 1) for p in range(2)]

    def build(c, spectrum):
        along = jnp.dot(
            spectrum[:, : cos_ref.shape[0]],
            cos_ref[...],
            precision=exact,
            preferred_element_type=jnp.float32,
        )
        strips = jnp.dot(
            turn_ref[...],
            jnp.concatenate([along * spread[p] for p in range(2)], 0),
            precision=exact,
            preferred_element_type=jnp.float32,
        )
        for parity in range(2):
            strip = strips[parity * half : (parity + 1) * half]

            lanes = strip.shape[1]
            turned = [
                pltpu.roll(strip, lanes - shift, 1) if shift else strip
                for shift in range(0, LANES, half)
            ]

            def window(start):
                base = start // LANES * LANES
                return turned[(start - base) // half][:, base : base + width]

            for x in range(half):
                toeplitz = window((size - 1 - x) * half)
                hankel = window(x * half)
                for sign in range(2):
                    value = toeplitz - hankel if sign else toeplitz + hankel
                    high, low = split_bf16(value)
                    high_ref[c, parity, sign, x * half : (x + 1) * half, :] = high
                    low_ref[c, parity, sign, x * half : (x + 1) * half, :] = low

    build(0, spectrum)

    table = jnp.concatenate([table_ref[...], table_ref[:, :LANES]], 1)
    values = lax.dot_general(
        table, operand, (((1,), (1,)), ((), ())), preferred_element_type=jnp.float32
    )
    for parity in range(2):
        part = values[:, parity * LANES : (parity + 1) * LANES]
        out_ref[:, parity] = part.reshape(size, 2 * group, LANES)

    @pl.when(pair == 0)
    def _():
        build(1, operator_spectrum(size, pair, 1, n_ky))


def gram_kernel(n_vec, n_grid, group, got_ref, high_ref, low_ref, out_ref):
    total = n_vec * group
    tile = 2 * group

    def apply(high, low, which):
        op_high, op_low = high_ref[which], low_ref[which]
        both = jnp.dot(
            jnp.concatenate([high, low], 0), op_high, preferred_element_type=jnp.float32
        )
        applied = both[: high.shape[0]] + both[high.shape[0] :]
        return applied + jnp.dot(high, op_low, preferred_element_type=jnp.float32)

    def gram_rows(one_operator):
        left, right = [], []
        for parity in range(2):
            slabs = []
            for i in range(n_grid):
                start = (i * 2 + parity) * tile
                rows = [
                    got_ref[pl.ds(start + row, n_vec, stride=n_grid * 2 * tile), :]
                    for row in range(tile)
                ]
                slabs.append(jnp.concatenate(rows, 0))
            for sign in range(2):
                folded = []
                for i in range(n_grid // 2):
                    near, far = slabs[i], slabs[n_grid - 1 - i]
                    folded.append(near - far if sign else near + far)
                high, low = split_bf16(jnp.concatenate(folded, 1))
                own = [slice(c * total, (c + 1) * total) for c in range(2)]
                if one_operator:
                    applied = apply(high, low, (0, parity, sign))
                else:
                    applied = jnp.concatenate(
                        [apply(high[own[c]], low[own[c]], (c, parity, sign)) for c in range(2)], 0
                    )
                applied_high, applied_low = split_bf16(applied)
                for rows in own:
                    left.append(jnp.concatenate([applied_high[rows], applied_low[rows]], 0))
                    right.append(jnp.concatenate([high[rows], low[rows]], 0))
        gram = lax.dot_general(
            jnp.concatenate(left, 1),
            jnp.concatenate(right, 1),
            (((1,), (1,)), ((), ())),
            preferred_element_type=jnp.float32,
        )
        gram = gram[:total] + gram[total:]
        gram = jnp.concatenate([gram, jnp.zeros((total, LANES - 2 * total), jnp.float32)], 1)
        for v in range(group):
            out_ref[pl.ds(v, n_vec, stride=group), :] = gram[v * n_vec : (v + 1) * n_vec]

    first = (lax.axis_index("vec") == 0) & (lax.axis_index("grid") == 0)

    @pl.when(first)
    def _():
        gram_rows(False)

    @pl.when(jnp.logical_not(first))
    def _():
        gram_rows(True)


def finish_kernel(n_vec, got_ref, out_ref):
    _, group, shifts = out_ref.shape
    total = n_vec * group
    g = lax.axis_index("vec")
    summed = jnp.sum(got_ref[...], 0, keepdims=True)
    lane = lax.broadcasted_iota(jnp.int32, summed.shape, 1)

    def from_lane(first):
        return pltpu.roll(summed, lax.rem(2 * LANES - first, LANES), 1)

    for w in range(group):
        start = w * n_vec + g
        ahead = from_lane(start) + from_lane(start + total)
        behind = from_lane(start - n_vec) + from_lane(start - n_vec + total)
        out_ref[0, w : w + 1, :] = jnp.where(lane < n_vec - g, ahead, behind)[:, :shifts]


def whole_blocks(count):
    return [pl.BlockSpec(memory_space=pltpu.VMEM)] * count


def tiled_program(fitting_vectors, size, n_vec, n_grid, shifts):
    group, slab, _ = fitting_vectors.shape
    half = size // 2
    n_devices = n_vec * n_grid
    total = n_vec * group
    spread = np.einsum("kcz,vw->kcvwz", pair_table(size), np.eye(group))
    high, low = split_table(spread.reshape(size * 2 * group, group * size))
    omega = math.pi / size
    freqs = np.arange(-(-(size + 1) // ROWS) * ROWS)
    offsets = np.arange(-(size - 1), half + 1)
    angle = omega * np.outer(freqs, centred(size)[:half])
    waves = np.stack([np.cos(angle), np.sin(angle)])
    waves[0, size] = 0.0
    waves[1, 0] = 0.0
    turn = np.einsum("pky,pq->pyqk", 0.5 * waves, np.eye(2))
    tables = [
        np.concatenate([high, low], 1),
        np.repeat(np.cos(omega * np.outer(freqs, offsets)), half, 1).astype(np.float32),
        np.tile(waves, (1, 1, LANES // half)).astype(np.float32),
        turn.reshape(2 * half, 2 * len(freqs)).astype(np.float32),
    ]
    op_shape = jax.ShapeDtypeStruct((2, 2, 2, half * half, half * half), jnp.bfloat16)
    arguments = [fitting_vectors] + [jnp.asarray(t) for t in tables]
    components, op_high, op_low = pl.pallas_call(
        functools.partial(prepare_kernel, size, n_grid),
        out_shape=(
            jax.ShapeDtypeStruct((size, 2, 2 * group, LANES), jnp.float32),
            op_shape,
            op_shape,
        ),
        in_specs=[pl.BlockSpec(memory_space=pltpu.HBM)] * len(arguments),
        out_specs=tuple(whole_blocks(3)),
        scratch_shapes=[pltpu.VMEM(a.shape, a.dtype) for a in arguments]
        + [
            pltpu.VMEM((2, half * slab, LANES), jnp.float32),
            pltpu.SemaphoreType.DMA((group + len(tables),)),
        ],
        compiler_params=PARAMS,
        name="prepare",
    )(*(pltpu.with_memory_space_constraint(a, pltpu.HBM) for a in arguments))
    got = lax.all_to_all(components, AXES, 0, 0, tiled=True)
    rows = pl.pallas_call(
        functools.partial(gram_kernel, n_vec, n_grid, group),
        out_shape=jax.ShapeDtypeStruct((total, LANES), jnp.float32),
        in_specs=whole_blocks(3),
        out_specs=whole_blocks(1)[0],
        compiler_params=PARAMS,
        name="gram",
    )(got.reshape(n_devices * 4 * group, LANES), op_high, op_low)
    parts = lax.all_to_all(rows, AXES, 0, 0, tiled=True)
    return pl.pallas_call(
        functools.partial(finish_kernel, n_vec),
        out_shape=jax.ShapeDtypeStruct((1, group, shifts), jnp.float32),
        in_specs=whole_blocks(1),
        out_specs=whole_blocks(1)[0],
        compiler_params=PARAMS,
        name="finish",
    )(parts).transpose(0, 2, 1)


def general_program(fitting_vectors, size, n_vec, n_grid, shifts):
    exact = lax.Precision.HIGHEST
    group, slab, _ = fitting_vectors.shape
    n_devices = n_vec * n_grid
    total = n_vec * group
    rank = lax.axis_index(AXES)
    sharers = max(1, n_devices // size)
    held = max(1, size // n_devices)
    components = jnp.einsum(
        "vxyz,kcz->kcvxy",
        fitting_vectors.reshape(group, slab, size, size),
        jnp.asarray(pair_table(size)),
        precision=exact,
    )
    chunks = jnp.repeat(components, sharers, 0)
    chunks = chunks.reshape(n_devices, held, 2, group, slab, size)
    got = lax.all_to_all(chunks, AXES, 0, 0, tiled=True)
    got = got.reshape(n_vec, n_grid, held, 2, group, slab, size)
    planes = got.transpose(2, 3, 0, 4, 1, 5, 6).reshape(held, 2, total, size * size)

    omega = math.pi / size
    cells = np.arange(size)
    steps = np.cos(
        omega * (cells[:, None, None] - cells[None, :, None]) * np.arange(size + 1)
    ).astype(np.float32)
    columns = size * size // sharers
    start = rank % sharers * columns
    gram = jnp.zeros((total, total), jnp.float32)
    for h in range(held):
        spectrum = pair_spectrum(size, rank // sharers * held + h)
        along = jnp.einsum("clk,xak->clxa", spectrum, steps, precision=exact)
        operator = jnp.einsum("ybl,clxa->cxyab", steps, along, precision=exact)
        operator = operator.reshape(2, size * size, size * size)
        operator = lax.dynamic_slice_in_dim(operator, start, columns, 2)
        applied = jnp.einsum("cmp,cpq->cmq", planes[h], operator, precision=exact)
        own = lax.dynamic_slice_in_dim(planes[h], start, columns, 2)
        gram += jnp.einsum("cmq,cnq->mn", applied, own, precision=exact)
    wanted = (np.arange(n_vec)[:, None] * group + np.arange(shifts * group)) % total
    wanted = np.repeat(wanted, group, 0)
    rows = jnp.take_along_axis(gram, jnp.asarray(wanted), 1)
    rows = rows.reshape(n_devices, total // n_devices, shifts * group)
    parts = lax.all_to_all(rows, AXES, 0, 0, tiled=True)
    return jnp.sum(parts, 0).reshape(total // n_devices, shifts, group)


def body(fitting_vectors):
    n_vec, n_grid = (lax.axis_size(a) for a in AXES)
    group, slab, plane = fitting_vectors.shape
    size = math.isqrt(plane)
    shifts = n_vec // 2 + 1
    tiled = (
        n_vec * n_grid == size
        and group * size == LANES
        and slab * size == 2 * LANES
        and 2 * group == ROWS
        and n_vec * group <= LANES
        and n_vec % 2 == 0
        and n_grid % 2 == 0
        and group == n_grid
    )
    build = tiled_program if tiled else general_program
    return build(fitting_vectors, size, n_vec, n_grid, shifts)


def solution(mesh):
    return jax.shard_map(
        body,
        mesh=mesh,
        in_specs=(P("vec", "grid", None),),
        out_specs=P(("vec", "grid"), None, None),
        check_vma=False,
    )
```

```python
import functools
import math

import jax
import jax.numpy as jnp
import numpy as np
from jax import lax
from jax.experimental import pallas as pl
from jax.experimental.pallas import tpu as pltpu
from jax.sharding import PartitionSpec as P

AXES = ("vec", "grid")
LANES = 128
ROWS = 8
PARAMS = pltpu.CompilerParams(vmem_limit_bytes=16 * 2**20)


def centred(size):
    return np.arange(size) - (size - 1) / 2


def pair_table(size):
    omega = math.pi / size
    freqs = np.arange(size)
    cosines = np.cos(omega * np.outer(freqs, centred(size)))
    sines = np.sin(omega * np.outer(np.where(freqs == 0, size, freqs), centred(size)))
    return np.stack([cosines, sines], 1).astype(np.float32)


def multiplicity(size):
    return np.where(np.isin(np.arange(size + 1), (0, size)), 1.0, 2.0)


def kernel_values(size, kz, ky, kx):
    total_sq = kz * kz + ky * ky + kx * kx
    wave_sq = total_sq * (math.pi / size) ** 2
    safe_sq = jnp.where(total_sq > 0, wave_sq, 1.0)
    half_arg = 0.5 * jnp.sqrt(safe_sq) * size
    values = 8.0 * math.pi * jnp.sin(half_arg) ** 2 / safe_sq
    return jnp.where(total_sq > 0, values, 2.0 * math.pi * size * size)


def times(size, k):
    inside = jnp.where((k == 0) | (k == size), 1.0, 2.0)
    return jnp.where(k <= size, inside, 0.0)


def scaled(size, values, pair, ky, kx):
    scale = 1.0 / (float(2 * size) ** 3 * float(size) ** 3)
    return values * times(size, ky) * times(size, kx) * jnp.where(pair == 0, scale, 2.0 * scale)


def operator_spectrum(size, pair, c, n_ky):
    ky = lax.broadcasted_iota(jnp.int32, (n_ky, LANES), 0)
    kx = lax.broadcasted_iota(jnp.int32, (n_ky, LANES), 1)
    kz = jnp.where(pair == 0, size, pair) if c else pair
    fz, fy, fx = (k.astype(jnp.float32) for k in (kz, ky, kx))
    return scaled(size, kernel_values(size, fz, fy, fx), pair, ky, kx)


def pair_spectrum(size, pair):
    kz = jnp.stack([pair, jnp.where(pair == 0, size, pair)])[:, None, None]
    ky = jnp.arange(size + 1, dtype=jnp.int32)[None, :, None]
    kx = jnp.arange(size + 1, dtype=jnp.int32)[None, None, :]
    fz, fy, fx = (k.astype(jnp.float32) for k in (kz, ky, kx))
    return scaled(size, kernel_values(size, fz, fy, fx), pair, ky, kx)


def split_bf16(value):
    high = value.astype(jnp.bfloat16)
    return high, (value - high.astype(jnp.float32)).astype(jnp.bfloat16)


def split_table(table):
    table = np.asarray(table, np.float32)
    high = table.astype(jnp.bfloat16)
    return high, (table - high.astype(np.float32)).astype(jnp.bfloat16)


def prepare_kernel(
    size,
    n_grid,
    field_hbm,
    table_hbm,
    cos_hbm,
    wave_hbm,
    turn_hbm,
    out_ref,
    high_ref,
    low_ref,
    field_ref,
    table_ref,
    cos_ref,
    wave_ref,
    turn_ref,
    held_ref,
    sems,
):
    group, slab, _ = field_ref.shape
    half = size // 2
    per_block = LANES // size
    blocks = size // per_block
    field_copies = [
        pltpu.make_async_copy(field_hbm.at[v], field_ref.at[v], sems.at[v]) for v in range(group)
    ]
    pairs = ((table_hbm, table_ref), (cos_hbm, cos_ref), (wave_hbm, wave_ref), (turn_hbm, turn_ref))
    table_copies = [
        pltpu.make_async_copy(source, target, sems.at[group + t])
        for t, (source, target) in enumerate(pairs)
    ]
    for copy in field_copies + table_copies:
        copy.start()
    n_ky = wave_ref.shape[1]
    pair = lax.axis_index("vec") * n_grid + lax.axis_index("grid")
    spectrum = operator_spectrum(size, pair, 0, n_ky)
    mirrored = lax.axis_index("grid") >= n_grid // 2
    lane_group = lax.broadcasted_iota(jnp.int32, (blocks * slab, LANES), 1) // size
    for copy in field_copies:
        copy.wait()
    stacked = [
        jnp.concatenate([field_ref[v, :, b * LANES : (b + 1) * LANES] for b in range(blocks)], 0)
        for v in range(group)
    ]
    turned = []
    for q in range(per_block):
        mixed = None
        for v in range(group):
            shift = (v - q) % per_block * size
            part = pltpu.roll(stacked[v], shift, 1) if shift else stacked[v]
            mixed = part if mixed is None else jnp.where(lane_group == v, part, mixed)
        turned.append(mixed)
    for y in range(half):
        b, q = divmod(y, per_block)
        other_b, other_q = divmod(size - 1 - y, per_block)
        near = turned[q][b * slab : (b + 1) * slab]
        far = turned[other_q][other_b * slab : (other_b + 1) * slab]
        held_ref[0, y * slab : (y + 1) * slab, :] = near + far
        held_ref[1, y * slab : (y + 1) * slab, :] = near - far
    rows = []
    for parity in range(2):
        for j in range(slab):
            start = jnp.where(mirrored, slab - 1 - j, j)
            rows.append(held_ref[parity, pl.ds(start, half, stride=slab), :])
    high, low = split_bf16(jnp.concatenate(rows, 0))
    operand = jnp.concatenate([high, high, low], 1)
    for copy in table_copies:
        copy.wait()
    width = half * half
    exact = lax.Precision.HIGHEST
    spread = [jnp.concatenate([wave_ref[p]] * (cos_ref.shape[1] // LANES), 1) for p in range(2)]

    def build(c, spectrum):
        along = jnp.dot(
            spectrum[:, : cos_ref.shape[0]],
            cos_ref[...],
            precision=exact,
            preferred_element_type=jnp.float32,
        )
        strips = jnp.dot(
            turn_ref[...],
            jnp.concatenate([along * spread[p] for p in range(2)], 0),
            precision=exact,
            preferred_element_type=jnp.float32,
        )
        for parity in range(2):
            strip = strips[parity * half : (parity + 1) * half]

            lanes = strip.shape[1]
            turned = [
                pltpu.roll(strip, lanes - shift, 1) if shift else strip
                for shift in range(0, LANES, half)
            ]

            def window(start):
                base = start // LANES * LANES
                return turned[(start - base) // half][:, base : base + width]

            for x in range(half):
                toeplitz = window((size - 1 - x) * half)
                hankel = window(x * half)
                for sign in range(2):
                    value = 0.5 * (toeplitz - hankel if sign else toeplitz + hankel)
                    high, low = split_bf16(value)
                    high_ref[c, parity, sign, x * half : (x + 1) * half, :] = high
                    low_ref[c, parity, sign, x * half : (x + 1) * half, :] = low

    build(0, spectrum)

    table = jnp.concatenate([table_ref[...], table_ref[:, :LANES]], 1)
    values = lax.dot_general(
        table, operand, (((1,), (1,)), ((), ())), preferred_element_type=jnp.float32
    )
    for parity in range(2):
        part = values[:, parity * LANES : (parity + 1) * LANES]
        out_ref[:, parity] = part.reshape(size, 2 * group, LANES)

    @pl.when(pair == 0)
    def _():
        build(1, operator_spectrum(size, pair, 1, n_ky))


def gram_kernel(n_vec, n_grid, group, got_ref, high_ref, low_ref, out_ref):
    total = n_vec * group
    tile = 2 * group

    def apply(high, low, which):
        op_high, op_low = high_ref[which], low_ref[which]
        both = jnp.dot(
            jnp.concatenate([high, low], 0), op_high, preferred_element_type=jnp.float32
        )
        applied = both[: high.shape[0]] + both[high.shape[0] :]
        return applied + jnp.dot(high, op_low, preferred_element_type=jnp.float32)

    def gram_rows(one_operator):
        left, right = [], []
        for parity in range(2):
            slabs = []
            for i in range(n_grid):
                start = (i * 2 + parity) * tile
                rows = [
                    got_ref[pl.ds(start + row, n_vec, stride=n_grid * 2 * tile), :]
                    for row in range(tile)
                ]
                slabs.append(jnp.concatenate(rows, 0))
            for sign in range(2):
                folded = []
                for i in range(n_grid // 2):
                    near, far = slabs[i], slabs[n_grid - 1 - i]
                    folded.append(near - far if sign else near + far)
                high, low = split_bf16(jnp.concatenate(folded, 1))
                own = [slice(c * total, (c + 1) * total) for c in range(2)]
                if one_operator:
                    applied = apply(high, low, (0, parity, sign))
                else:
                    applied = jnp.concatenate(
                        [apply(high[own[c]], low[own[c]], (c, parity, sign)) for c in range(2)], 0
                    )
                applied_high, applied_low = split_bf16(applied)
                for rows in own:
                    left.append(jnp.concatenate([applied_high[rows], applied_low[rows]], 0))
                    right.append(jnp.concatenate([high[rows], low[rows]], 0))
        gram = lax.dot_general(
            jnp.concatenate(left, 1),
            jnp.concatenate(right, 1),
            (((1,), (1,)), ((), ())),
            preferred_element_type=jnp.float32,
        )
        gram = gram[:total] + gram[total:]
        gram = jnp.concatenate([gram, jnp.zeros((total, LANES - 2 * total), jnp.float32)], 1)
        for v in range(group):
            out_ref[pl.ds(v, n_vec, stride=group), :] = gram[v * n_vec : (v + 1) * n_vec]

    first = (lax.axis_index("vec") == 0) & (lax.axis_index("grid") == 0)

    @pl.when(jnp.logical_not(first))
    def _():
        gram_rows(True)

    @pl.when(first)
    def _():
        gram_rows(False)


def finish_kernel(n_vec, got_ref, out_ref):
    _, group, shifts = out_ref.shape
    total = n_vec * group
    g = lax.axis_index("vec")
    summed = jnp.sum(got_ref[...], 0, keepdims=True)
    lane = lax.broadcasted_iota(jnp.int32, summed.shape, 1)

    def from_lane(first):
        return pltpu.roll(summed, lax.rem(2 * LANES - first, LANES), 1)

    for w in range(group):
        start = w * n_vec + g
        ahead = from_lane(start) + from_lane(start + total)
        behind = from_lane(start - n_vec) + from_lane(start - n_vec + total)
        out_ref[0, w : w + 1, :] = jnp.where(lane < n_vec - g, ahead, behind)[:, :shifts]


def whole_blocks(count):
    return [pl.BlockSpec(memory_space=pltpu.VMEM)] * count


def tiled_program(fitting_vectors, size, n_vec, n_grid, shifts):
    group, slab, _ = fitting_vectors.shape
    half = size // 2
    n_devices = n_vec * n_grid
    total = n_vec * group
    spread = np.einsum("kcz,vw->kcvwz", pair_table(size), np.eye(group))
    high, low = split_table(spread.reshape(size * 2 * group, group * size))
    omega = math.pi / size
    freqs = np.arange(-(-(size + 1) // ROWS) * ROWS)
    offsets = np.arange(-(size - 1), half + 1)
    angle = omega * np.outer(freqs, centred(size)[:half])
    waves = np.stack([np.cos(angle), np.sin(angle)])
    waves[0, size] = 0.0
    waves[1, 0] = 0.0
    turn = np.einsum("pky,pq->pyqk", waves, np.eye(2))
    tables = [
        np.concatenate([high, low], 1),
        np.repeat(np.cos(omega * np.outer(freqs, offsets)), half, 1).astype(np.float32),
        np.tile(waves, (1, 1, LANES // half)).astype(np.float32),
        turn.reshape(2 * half, 2 * len(freqs)).astype(np.float32),
    ]
    op_shape = jax.ShapeDtypeStruct((2, 2, 2, half * half, half * half), jnp.bfloat16)
    arguments = [fitting_vectors] + [jnp.asarray(t) for t in tables]
    components, op_high, op_low = pl.pallas_call(
        functools.partial(prepare_kernel, size, n_grid),
        out_shape=(
            jax.ShapeDtypeStruct((size, 2, 2 * group, LANES), jnp.float32),
            op_shape,
            op_shape,
        ),
        in_specs=[pl.BlockSpec(memory_space=pltpu.HBM)] * len(arguments),
        out_specs=tuple(whole_blocks(3)),
        scratch_shapes=[pltpu.VMEM(a.shape, a.dtype) for a in arguments]
        + [
            pltpu.VMEM((2, half * slab, LANES), jnp.float32),
            pltpu.SemaphoreType.DMA((group + len(tables),)),
        ],
        compiler_params=PARAMS,
        name="prepare",
    )(*(pltpu.with_memory_space_constraint(a, pltpu.HBM) for a in arguments))
    got = lax.all_to_all(components, AXES, 0, 0, tiled=True)
    rows = pl.pallas_call(
        functools.partial(gram_kernel, n_vec, n_grid, group),
        out_shape=jax.ShapeDtypeStruct((total, LANES), jnp.float32),
        in_specs=whole_blocks(3),
        out_specs=whole_blocks(1)[0],
        compiler_params=PARAMS,
        name="gram",
    )(got.reshape(n_devices * 4 * group, LANES), op_high, op_low)
    parts = lax.all_to_all(rows, AXES, 0, 0, tiled=True)
    return pl.pallas_call(
        functools.partial(finish_kernel, n_vec),
        out_shape=jax.ShapeDtypeStruct((1, group, shifts), jnp.float32),
        in_specs=whole_blocks(1),
        out_specs=whole_blocks(1)[0],
        compiler_params=PARAMS,
        name="finish",
    )(parts).transpose(0, 2, 1)


def general_program(fitting_vectors, size, n_vec, n_grid, shifts):
    exact = lax.Precision.HIGHEST
    group, slab, _ = fitting_vectors.shape
    n_devices = n_vec * n_grid
    total = n_vec * group
    rank = lax.axis_index(AXES)
    sharers = max(1, n_devices // size)
    held = max(1, size // n_devices)
    components = jnp.einsum(
        "vxyz,kcz->kcvxy",
        fitting_vectors.reshape(group, slab, size, size),
        jnp.asarray(pair_table(size)),
        precision=exact,
    )
    chunks = jnp.repeat(components, sharers, 0)
    chunks = chunks.reshape(n_devices, held, 2, group, slab, size)
    got = lax.all_to_all(chunks, AXES, 0, 0, tiled=True)
    got = got.reshape(n_vec, n_grid, held, 2, group, slab, size)
    planes = got.transpose(2, 3, 0, 4, 1, 5, 6).reshape(held, 2, total, size * size)

    omega = math.pi / size
    cells = np.arange(size)
    steps = np.cos(
        omega * (cells[:, None, None] - cells[None, :, None]) * np.arange(size + 1)
    ).astype(np.float32)
    columns = size * size // sharers
    start = rank % sharers * columns
    gram = jnp.zeros((total, total), jnp.float32)
    for h in range(held):
        spectrum = pair_spectrum(size, rank // sharers * held + h)
        along = jnp.einsum("clk,xak->clxa", spectrum, steps, precision=exact)
        operator = jnp.einsum("ybl,clxa->cxyab", steps, along, precision=exact)
        operator = operator.reshape(2, size * size, size * size)
        operator = lax.dynamic_slice_in_dim(operator, start, columns, 2)
        applied = jnp.einsum("cmp,cpq->cmq", planes[h], operator, precision=exact)
        own = lax.dynamic_slice_in_dim(planes[h], start, columns, 2)
        gram += jnp.einsum("cmq,cnq->mn", applied, own, precision=exact)
    wanted = (np.arange(n_vec)[:, None] * group + np.arange(shifts * group)) % total
    wanted = np.repeat(wanted, group, 0)
    rows = jnp.take_along_axis(gram, jnp.asarray(wanted), 1)
    rows = rows.reshape(n_devices, total // n_devices, shifts * group)
    parts = lax.all_to_all(rows, AXES, 0, 0, tiled=True)
    return jnp.sum(parts, 0).reshape(total // n_devices, shifts, group)


def body(fitting_vectors):
    n_vec, n_grid = (lax.axis_size(a) for a in AXES)
    group, slab, plane = fitting_vectors.shape
    size = math.isqrt(plane)
    shifts = n_vec // 2 + 1
    tiled = (
        n_vec * n_grid == size
        and group * size == LANES
        and slab * size == 2 * LANES
        and 2 * group == ROWS
        and n_vec * group <= LANES
        and n_vec % 2 == 0
        and n_grid % 2 == 0
        and group == n_grid
    )
    build = tiled_program if tiled else general_program
    return build(fitting_vectors, size, n_vec, n_grid, shifts)


def solution(mesh):
    return jax.shard_map(
        body,
        mesh=mesh,
        in_specs=(P("vec", "grid", None),),
        out_specs=P(("vec", "grid"), None, None),
        check_vma=False,
    )
```
